32 devices in a mesh: grp: 2 (over x), fsdp: 8 (over z, y), tp: 2 (over core).
Axes of the slice: x: 2, y: 2, z: 4, core: 2. Of those that a mesh axis runs over, the one named last changes fastest.
Arguments:
- hidden: bfloat16 [256, 2, 5120], P('grp', None, 'fsdp'), parts along dimension 0, may hold values from -90 to 90
- input_gain: float32 [5120], P('fsdp'), may hold values from 0.3 to 3
- q_gain: float32 [128], replicated, may hold values from 0.5 to 2.5
- k_gain: float32 [128], replicated, may hold values from 0.5 to 2.5
- base_qkv: bfloat16 [10240, 5120], P('tp', 'fsdp'), may hold values from -0.078125 to 0.078125
- codes_qkv: bfloat16 [10240, 5120], P(('tp', 'fsdp')), may hold values from -448 to 448
- scale_qkv: float32 [80, 40], replicated, may hold values from 2e-05 to 0.0002
- base_out: bfloat16 [5120, 8192], P('fsdp', 'tp'), may hold values from -0.125 to 0.125
- codes_out: bfloat16 [5120, 8192], P(('fsdp', 'tp')), may hold values from -448 to 448
- scale_out: float32 [40, 64], replicated, may hold values from 2e-05 to 0.0002
- lengths: int32 [256], P(('grp', 'fsdp')), parts along dimension 0, may hold values from 1 to 512, as said below
- key_cache: bfloat16 [256, 512, 8, 128], P(('grp', 'fsdp'), None, 'tp'), parts along dimension 0, may hold values from -2.5 to 2.5
- value_cache: bfloat16 [256, 512, 8, 128], P(('grp', 'fsdp'), None, 'tp'), parts along dimension 0, may hold values from -2.5 to 2.5
Outputs:
- decoded: bfloat16 [256, 2, 5120], P('grp', None, 'fsdp'), parts along dimension 0
The draws below stay inside these ranges and needn't reach their ends.
There are 2 independent parts, one for each index of `grp`. The reference program is written for one: setup_inputs(seed, part) draws one part's arguments, and reference() takes and returns one part's arrays. A program takes and returns all parts, laid end to end along the dimension named above; an argument that names none is the same for every part. Nothing has to cross between parts.
Inputs may be any that keep to these rules, and one draw needn't show every extreme that they name: Keys and values of a row at positions of lengths or more are not read; some row has exactly 512.
All inputs are finite; a program needn't handle non-finite values.
Results may differ from the reference program's by a relative error of at most 0.005.
The reference program's roundings to bfloat16 on the way count: a program that leaves them out, or rounds other values in their place, can miss the bound.
Values may be sent and summed in bfloat16 or wider, within the bound.
A program may use at most 192 MiB of HBM per device.

```python
import math
import jax
import jax.numpy as jnp
from jax import lax

D = 5120
HQ = 64
KVH = 8
HD = 128
BLOCK = 128
CACHE = 512
QKV = 10240
ROWS = 128


def draw_hidden(key, part):
    key = jax.random.fold_in(key, 11)
    key_values, key_columns = jax.random.split(key)
    column_rise = jnp.exp(jnp.arange(D).astype(jnp.float32) * (math.log(3.0) / D))
    base_values = jax.random.truncated_normal(key_values, -4.0, 4.0, (ROWS, 2, D), jnp.float32)
    column_spread = jnp.exp(jax.random.uniform(key_columns, (D,), jnp.float32, 0.0, math.log(10.0)))
    return (base_values * column_rise * column_spread * 0.25).astype(jnp.bfloat16)


def draw_lengths(key, part):
    key = jax.random.fold_in(key, 23)
    key_lengths, key_chosen = jax.random.split(key)
    drawn = jax.random.randint(key_lengths, (ROWS,), 1, CACHE + 1, dtype=jnp.int32)
    chosen = jax.random.randint(key_chosen, (), 0, ROWS, dtype=jnp.int32)
    return jnp.where(jnp.arange(ROWS, dtype=jnp.int32) == chosen, CACHE, drawn).astype(jnp.int32)


def levels(stream_key, extent, cuts, least, largest):
    loudness = 1.0
    for axis_at, blocks in cuts:
        steps = jax.random.uniform(jax.random.fold_in(jax.random.fold_in(stream_key, 6), axis_at), (blocks,), jnp.float32, least / len(cuts), largest / len(cuts))
        loudness = loudness * jnp.repeat(jnp.exp(steps), extent[axis_at] // blocks).reshape((-1,) + (1,) * (len(extent) - 1 - axis_at))
    return loudness


def centred(key, extent, spread, bound, shards=(), kind=jnp.bfloat16):
    entries = jax.random.normal(key, extent, jnp.float32) * spread
    if len(shards) > 0:
        entries = levels(key, extent, shards, -0.22, 0.18) * entries
    return jnp.clip(entries, min=-bound, max=bound).astype(kind)


def setup_inputs(seed: int = 0, part: int = 0) -> dict:
    arg_keys = jax.random.split(jax.random.key(seed), 14)
    part_keys = jax.random.split(jax.random.fold_in(arg_keys[13], part), 14)
    return {
        "hidden": draw_hidden(jax.random.fold_in(jax.random.fold_in(arg_keys[13], part), 71), part),
        "input_gain": jnp.clip(jnp.exp(math.log(3.0) - 2.3025851 * jax.random.uniform(arg_keys[1], (D,), jnp.float32) ** levels(arg_keys[1], (D,), ((0, 8),), -0.2, 0.2)), 0.3, 3.0),
        "q_gain": jnp.clip(jnp.exp(jax.random.uniform(arg_keys[2], (HD,), jnp.float32, math.log(0.5), math.log(2.5))), 0.5, 2.5),
        "k_gain": jnp.clip(jnp.exp(jax.random.uniform(arg_keys[3], (HD,), jnp.float32, math.log(0.5), math.log(2.5))), 0.5, 2.5),
        "base_qkv": centred(arg_keys[4], (QKV, D), D ** -0.5, 0.078125, ((0, 2), (1, 8))),
        "codes_qkv": centred(arg_keys[5], (QKV, D), 100.0, 448.0, ((0, 16),)),
        "scale_qkv": jnp.clip(jnp.exp(jax.random.uniform(arg_keys[6], (QKV // BLOCK, D // BLOCK), jnp.float32, math.log(1.9999999494757503e-05), math.log(0.0002))), 1.9999999494757503e-05, 0.0002),
        "base_out": centred(arg_keys[7], (D, HQ * HD), (HQ * HD // 4) ** -0.5, 0.125, ((0, 8), (1, 2))),
        "codes_out": centred(arg_keys[8], (D, HQ * HD), 100.0, 448.0, ((0, 16),)),
        "scale_out": jnp.clip(jnp.exp(jax.random.uniform(arg_keys[9], (D // BLOCK, HQ * HD // BLOCK), jnp.float32, math.log(1.9999999494757503e-05), math.log(0.0002))), 1.9999999494757503e-05, 0.0002),
        "lengths": draw_lengths(jax.random.fold_in(jax.random.fold_in(arg_keys[13], part), 71), part),
        "key_cache": centred(part_keys[11], (ROWS, CACHE, KVH, HD), 1.0, 2.5, ((0, 8), (2, 2))),
        "value_cache": centred(part_keys[12], (ROWS, CACHE, KVH, HD), 1.0, 2.5, ((0, 8), (2, 2))),
    }


epsilon = 1e-06
rope_base = 1000000.0

def dequantize(base, codes, scale):
    expanded = jnp.repeat(jnp.repeat(scale, BLOCK, axis=0), BLOCK, axis=1)
    return (base.astype(jnp.float32) + codes.astype(jnp.float32) * expanded).astype(jnp.bfloat16)

def head_norm(values, gain):
    return values * lax.rsqrt(lax.optimization_barrier(jnp.mean(values * values, axis=-1, keepdims=True)) + epsilon) * gain

def rotate(values, positions):
    half_dim = values.shape[-1] // 2
    frequency = jnp.exp(jnp.arange(half_dim).astype(jnp.float32) * (-2.0 * math.log(rope_base) / values.shape[-1]))
    angles = positions.astype(jnp.float32)[..., None] * frequency
    angles = angles.reshape(positions.shape + (1,) * (values.ndim - positions.ndim - 1) + (half_dim,))
    cosine = jnp.cos(angles)
    sine_part = jnp.sin(angles)
    first_part = values[..., :half_dim]
    second_part = values[..., half_dim:]
    return jnp.concatenate([first_part * cosine - second_part * sine_part, second_part * cosine + first_part * sine_part], axis=-1)

def attend(projected, lengths, key_cache, value_cache, q_gain, k_gain):
    row_count = projected.shape[0]
    groups = key_cache.shape[2]
    head_dim = key_cache.shape[3]
    grouped = projected.reshape(row_count, 2, groups, -1, head_dim)
    per_group = grouped.shape[3]
    queries = grouped[:, :, :, :per_group - 2]
    new_keys = grouped[:, :, :, per_group - 2]
    new_values = grouped[:, :, :, per_group - 1].astype(jnp.bfloat16)
    positions = lengths[:, None] + jnp.arange(2, dtype=jnp.int32)[None, :]
    queries = rotate(head_norm(queries, q_gain), positions).astype(jnp.bfloat16)
    new_keys = rotate(head_norm(new_keys, k_gain), positions).astype(jnp.bfloat16)
    scaling = 1.0 / math.sqrt(head_dim)
    cache_scores = jnp.einsum('rsgqd,rlgd->rsgql', queries.astype(jnp.float32), key_cache.astype(jnp.float32)) * scaling
    new_scores = jnp.einsum('rsgqd,rtgd->rsgqt', queries.astype(jnp.float32), new_keys.astype(jnp.float32)) * scaling
    cache_mask = (jnp.arange(key_cache.shape[1], dtype=jnp.int32)[None, :] < lengths[:, None]).reshape(row_count, 1, 1, 1, -1)
    step_mask = (jnp.arange(2, dtype=jnp.int32)[None, :] <= jnp.arange(2, dtype=jnp.int32)[:, None]).reshape(1, 2, 1, 1, 2)
    cache_weights = jnp.where(cache_mask, jnp.exp(cache_scores), 0.0)
    new_weights = jnp.where(step_mask, jnp.exp(new_scores), 0.0)
    totals = lax.optimization_barrier(jnp.sum(cache_weights, axis=-1)) + lax.optimization_barrier(jnp.sum(new_weights, axis=-1))
    cache_weights = (cache_weights / totals[..., None]).astype(jnp.bfloat16)
    new_weights = (new_weights / totals[..., None]).astype(jnp.bfloat16)
    mixed = jnp.einsum('rsgql,rlgd->rsgqd', cache_weights.astype(jnp.float32), value_cache.astype(jnp.float32))
    mixed = mixed + jnp.einsum('rsgqt,rtgd->rsgqd', new_weights.astype(jnp.float32), new_values.astype(jnp.float32))
    return mixed.reshape(row_count, 2, -1).astype(jnp.bfloat16)

def reference(hidden, input_gain, q_gain, k_gain, base_qkv, codes_qkv, scale_qkv, base_out, codes_out, scale_out, lengths, key_cache, value_cache):
    new_qkv = dequantize(base_qkv, codes_qkv, scale_qkv)
    new_out = dequantize(base_out, codes_out, scale_out)
    hidden_float = hidden.astype(jnp.float32)
    mean_square = lax.optimization_barrier(jnp.sum(hidden_float * hidden_float, axis=-1)) / D
    normed = (hidden_float * lax.rsqrt(mean_square + epsilon)[..., None] * input_gain).astype(jnp.bfloat16)
    projected = jnp.dot(normed.reshape(-1, D), new_qkv.T, preferred_element_type=jnp.float32)
    projected = projected.reshape(ROWS, 2, -1)
    attended = attend(projected, lengths, key_cache, value_cache, q_gain, k_gain)
    decoded = jnp.dot(attended.reshape(ROWS * 2, -1), new_out.T, preferred_element_type=jnp.float32)
    return decoded.reshape(ROWS, 2, D).astype(jnp.bfloat16)
```

```python
import functools
import math

import jax
import jax.numpy as jnp
from jax import lax
from jax.experimental import pallas as pl
from jax.experimental.pallas import tpu as pltpu
from jax.sharding import PartitionSpec as P

D = 5120
BLOCK = 128


epsilon = 1e-06
rope_base = 1000000.0


def head_norm(values, gain):
    return values * lax.rsqrt(jnp.mean(values * values, axis=-1, keepdims=True) + epsilon) * gain


def rotate(values, positions):
    half_dim = values.shape[-1] // 2
    frequency = jnp.exp(
        jnp.arange(half_dim).astype(jnp.float32) * (-2.0 * math.log(rope_base) / values.shape[-1])
    )
    angles = positions.astype(jnp.float32)[..., None] * frequency
    angles = angles.reshape(
        positions.shape + (1,) * (values.ndim - positions.ndim - 1) + (half_dim,)
    )
    cosine = jnp.cos(angles)
    sine_part = jnp.sin(angles)
    first_part = values[..., :half_dim]
    second_part = values[..., half_dim:]
    return jnp.concatenate(
        [
            first_part * cosine - second_part * sine_part,
            second_part * cosine + first_part * sine_part,
        ],
        axis=-1,
    )


def attend(projected, lengths, key_cache, value_cache, q_gain, k_gain):
    row_count = projected.shape[0]
    groups = key_cache.shape[2]
    head_dim = key_cache.shape[3]
    grouped = projected.reshape(row_count, 2, groups, -1, head_dim)
    per_group = grouped.shape[3]
    queries = grouped[:, :, :, : per_group - 2]
    new_keys = grouped[:, :, :, per_group - 2]
    new_values = grouped[:, :, :, per_group - 1].astype(jnp.bfloat16)
    positions = lengths[:, None] + jnp.arange(2, dtype=jnp.int32)[None, :]
    queries = rotate(head_norm(queries, q_gain), positions).astype(jnp.bfloat16)
    new_keys = rotate(head_norm(new_keys, k_gain), positions).astype(jnp.bfloat16)
    scaling = 1.0 / math.sqrt(head_dim)
    cache_scores = (
        jnp.einsum("rsgqd,rlgd->rsgql", queries, key_cache, preferred_element_type=jnp.float32)
        * scaling
    )
    new_scores = (
        jnp.einsum("rsgqd,rtgd->rsgqt", queries, new_keys, preferred_element_type=jnp.float32)
        * scaling
    )
    cache_mask = (
        jnp.arange(key_cache.shape[1], dtype=jnp.int32)[None, :] < lengths[:, None]
    ).reshape(row_count, 1, 1, 1, -1)
    step_mask = (
        jnp.arange(2, dtype=jnp.int32)[None, :] <= jnp.arange(2, dtype=jnp.int32)[:, None]
    ).reshape(1, 2, 1, 1, 2)
    cache_weights = jnp.where(cache_mask, jnp.exp(cache_scores), 0.0)
    new_weights = jnp.where(step_mask, jnp.exp(new_scores), 0.0)
    totals = jnp.sum(cache_weights, axis=-1) + jnp.sum(new_weights, axis=-1)
    cache_weights = (cache_weights / totals[..., None]).astype(jnp.bfloat16)
    new_weights = (new_weights / totals[..., None]).astype(jnp.bfloat16)
    mixed = jnp.einsum(
        "rsgql,rlgd->rsgqd", cache_weights, value_cache, preferred_element_type=jnp.float32
    )
    mixed = mixed + jnp.einsum(
        "rsgqt,rtgd->rsgqd", new_weights, new_values, preferred_element_type=jnp.float32
    )
    return mixed.reshape(row_count, 2, -1).astype(jnp.bfloat16)


MESH = pl.DeviceIdType.MESH
ANY = pl.BlockSpec(memory_space=pl.ANY)


def greet(axes):
    barrier = pltpu.get_barrier_semaphore()
    total = 0
    for axis in axes:
        size = lax.axis_size(axis)
        me = lax.axis_index(axis)
        for step in range(1, size):
            pl.semaphore_signal(
                barrier, inc=1, device_id={axis: lax.rem(me + step, size)}, device_id_type=MESH
            )
        total += size - 1
    pl.semaphore_wait(barrier, total)


def columns_at(index, width):
    start = index * width
    return pl.ds(pl.multiple_of(start, 128) if width % 128 == 0 else start, width)


def landing(ref, split, rows, index, width):
    if split:
        return ref.at[index, rows]
    return ref.at[rows, columns_at(index, width)]


def relay_kernel(split, base, codes, got_base, got_codes, s_base, r_base, s_fwd, r_fwd, s_code, r_code, s_local):
    groups, shards, halves = lax.axis_size("grp"), lax.axis_size("fsdp"), lax.axis_size("tp")
    grp, fsdp, tp = lax.axis_index("grp"), lax.axis_index("fsdp"), lax.axis_index("tp")
    width = base.shape[1]
    rows = base.shape[0] // shards
    part = rows // groups
    code_rows = codes.shape[0]
    code_width = codes.shape[1] // halves
    greet(("grp", "fsdp", "tp"))
    mine = pl.ds(pl.multiple_of(grp * part, 16), part)
    started = []
    base_copies = {}
    for step in range(1, shards):
        peer = lax.rem(fsdp + step, shards)
        copy = pltpu.make_async_remote_copy(
            src_ref=base.at[pl.ds(pl.multiple_of(peer * rows + grp * part, 16), part)],
            dst_ref=landing(got_base, split, mine, fsdp, width),
            send_sem=s_base.at[step],
            recv_sem=r_base.at[step],
            device_id={"fsdp": peer},
            device_id_type=MESH,
        )
        copy.start()
        base_copies[step] = copy
    own_rows = pl.ds(pl.multiple_of(tp * code_rows, 16), code_rows)
    for step in range(1, halves):
        peer = lax.rem(tp + step, halves)
        copy = pltpu.make_async_remote_copy(
            src_ref=codes.at[:, columns_at(peer, code_width)],
            dst_ref=got_codes.at[own_rows],
            send_sem=s_code.at[step],
            recv_sem=r_code.at[step],
            device_id={"tp": peer},
            device_id_type=MESH,
        )
        copy.start()
        started.append(copy)
    local_codes = pltpu.make_async_copy(
        codes.at[:, columns_at(tp, code_width)], got_codes.at[own_rows], s_local.at[0]
    )
    local_codes.start()
    local_base = pltpu.make_async_copy(
        base.at[pl.ds(pl.multiple_of(fsdp * rows, 16), rows)],
        landing(got_base, split, pl.ds(0, rows), fsdp, width),
        s_local.at[1],
    )
    local_base.start()
    for step in range(1, shards):
        base_copies[step].wait_recv()
        source = lax.rem(fsdp + shards - step, shards)
        for hop in range(1, groups):
            block = landing(got_base, split, mine, source, width)
            copy = pltpu.make_async_remote_copy(
                src_ref=block,
                dst_ref=block,
                send_sem=s_fwd.at[step, hop],
                recv_sem=r_fwd.at[step, hop],
                device_id={"grp": lax.rem(grp + hop, groups)},
                device_id_type=MESH,
            )
            copy.start()
            started.append(copy)
    for step in range(1, shards):
        base_copies[step].wait_send()
    for copy in started:
        copy.wait()
    local_codes.wait()
    local_base.wait()


def relay(base, codes, grp_size, shards, halves):
    width = base.shape[1]
    rows = base.shape[0] // shards
    split = width % 128 != 0
    base_shape = (shards, rows, width) if split else (rows, shards * width)
    dma = pltpu.SemaphoreType.DMA
    got_base, got_codes = pl.pallas_call(
        functools.partial(relay_kernel, split),
        out_shape=(
            jax.ShapeDtypeStruct(base_shape, base.dtype),
            jax.ShapeDtypeStruct((codes.shape[0] * halves, codes.shape[1] // halves), codes.dtype),
        ),
        in_specs=[ANY, ANY],
        out_specs=(ANY, ANY),
        scratch_shapes=[
            dma((shards,)), dma((shards,)),
            dma((shards, grp_size)), dma((shards, grp_size)),
            dma((halves,)), dma((halves,)), dma((2,)),
        ],
        compiler_params=pltpu.CompilerParams(collective_id=0, has_side_effects=True),
        cost_estimate=pl.CostEstimate(flops=0, bytes_accessed=250_000_000, transcendentals=0),
        name="relay",
    )(base, codes)
    if split:
        got_base = jnp.swapaxes(got_base, 0, 1).reshape(rows, shards * width)
    return got_base, got_codes


def to_rows_kernel(split, values, got, s_sem, r_sem, s_local):
    shards = lax.axis_size("fsdp")
    fsdp = lax.axis_index("fsdp")
    rows = values.shape[0] // shards
    width = values.shape[1]
    greet(("fsdp",))
    every = pl.ds(0, rows)
    copies = []
    for step in range(1, shards):
        peer = lax.rem(fsdp + step, shards)
        copy = pltpu.make_async_remote_copy(
            src_ref=values.at[pl.ds(pl.multiple_of(peer * rows, 8), rows)],
            dst_ref=landing(got, split, every, fsdp, width),
            send_sem=s_sem.at[step],
            recv_sem=r_sem.at[step],
            device_id={"fsdp": peer},
            device_id_type=MESH,
        )
        copy.start()
        copies.append(copy)
    local = pltpu.make_async_copy(
        values.at[pl.ds(pl.multiple_of(fsdp * rows, 8), rows)],
        landing(got, split, every, fsdp, width),
        s_local,
    )
    local.start()
    for copy in copies:
        copy.wait()
    local.wait()


def to_rows(values, shards):
    rows = values.shape[0] // shards
    width = values.shape[1]
    split = width % 128 != 0
    dma = pltpu.SemaphoreType.DMA
    got = pl.pallas_call(
        functools.partial(to_rows_kernel, split),
        out_shape=jax.ShapeDtypeStruct(
            (shards, rows, width) if split else (rows, shards * width), values.dtype
        ),
        in_specs=[ANY],
        out_specs=ANY,
        scratch_shapes=[dma((shards,)), dma((shards,)), dma],
        compiler_params=pltpu.CompilerParams(collective_id=1, has_side_effects=True),
        name="to_rows",
    )(values)
    if split:
        got = jnp.swapaxes(got, 0, 1).reshape(rows, shards * width)
    return got


def updated_matmul_kernel(x, base, codes, scale, out):
    depth = x.shape[1]

    @pl.when(pl.program_id(0) == 0)
    def _():
        out[...] = jnp.zeros_like(out)

    parts = []
    for block in range(depth // BLOCK):
        at = slice(block * BLOCK, (block + 1) * BLOCK)
        delta = codes[:, at].astype(jnp.float32) * scale[0, :, block : block + 1]
        parts.append((base[:, at].astype(jnp.float32) + delta).astype(jnp.bfloat16))
    out[...] += lax.dot_general(
        x[...], jnp.concatenate(parts, axis=1), (((1,), (1,)), ((), ())),
        preferred_element_type=jnp.float32,
    )


def updated_matmul(x, base, codes, row_scale, depth=512):
    count, total = base.shape
    steps = total // depth
    scale = row_scale.reshape(count, steps, depth // BLOCK).transpose(1, 0, 2)
    return pl.pallas_call(
        updated_matmul_kernel,
        grid=(steps,),
        out_shape=jax.ShapeDtypeStruct((x.shape[0], count), jnp.float32),
        in_specs=[
            pl.BlockSpec((x.shape[0], depth), lambda i: (0, i)),
            pl.BlockSpec((count, depth), lambda i: (0, i)),
            pl.BlockSpec((count, depth), lambda i: (0, i)),
            pl.BlockSpec((1, count, depth // BLOCK), lambda i: (i, 0, 0)),
        ],
        out_specs=pl.BlockSpec((x.shape[0], count), lambda i: (0, 0)),
        compiler_params=pltpu.CompilerParams(vmem_limit_bytes=24 * 2**20),
        cost_estimate=pl.CostEstimate(
            flops=2 * x.shape[0] * count * total, bytes_accessed=4 * count * total, transcendentals=0
        ),
        name="updated_matmul",
    )(x, base, codes, scale)


def row_scales(scale, first_row, rows):
    ids = (first_row + jnp.arange(rows, dtype=jnp.int32)) // BLOCK
    pick = (ids[:, None] == jnp.arange(scale.shape[0], dtype=jnp.int32)[None, :]).astype(jnp.float32)
    return jnp.dot(pick, scale, precision=lax.Precision.HIGHEST)


def on_device(
    hidden,
    input_gain,
    q_gain,
    k_gain,
    base_qkv,
    codes_qkv,
    scale_qkv,
    base_out,
    codes_out,
    scale_out,
    lengths,
    key_cache,
    value_cache,
):
    grp_size, shards, halves = lax.axis_size("grp"), lax.axis_size("fsdp"), lax.axis_size("tp")
    fsdp_index = lax.axis_index("fsdp")
    tp_index = lax.axis_index("tp")
    row_count = hidden.shape[0]
    whole_hidden = lax.all_gather(hidden.reshape(row_count * 2, -1), "fsdp", axis=1, tiled=True)
    whole_gain = lax.all_gather(input_gain, "fsdp", axis=0, tiled=True)
    arrived_base, arrived_out = relay(base_qkv, codes_out, grp_size, shards, halves)

    hidden_float = whole_hidden.astype(jnp.float32)
    mean_square = jnp.sum(hidden_float * hidden_float, axis=-1) / D
    normed = (hidden_float * lax.rsqrt(mean_square + epsilon)[..., None] * whole_gain).astype(
        jnp.bfloat16
    )
    qkv_rows = codes_qkv.shape[0]
    qkv_scale = row_scales(scale_qkv, (tp_index * shards + fsdp_index) * qkv_rows, qkv_rows)
    projected = updated_matmul(normed, arrived_base, codes_qkv, qkv_scale)
    projected = to_rows(projected, shards).reshape(row_count // shards, 2, -1)
    attended = attend(projected, lengths, key_cache, value_cache, q_gain, k_gain)

    out_rows, out_columns = base_out.shape
    column_blocks = out_columns // BLOCK
    scale_columns = lax.dynamic_slice_in_dim(scale_out, tp_index * column_blocks, column_blocks, 1)
    out_scale = row_scales(scale_columns, fsdp_index * out_rows, out_rows)
    whole_attended = lax.all_gather(
        attended.reshape(-1, attended.shape[-1]), "fsdp", axis=0, tiled=True
    )
    partial_out = updated_matmul(whole_attended, base_out, arrived_out, out_scale)
    return lax.psum(partial_out, "tp").astype(jnp.bfloat16).reshape(row_count, 2, out_rows)


def solution(mesh):
    return jax.shard_map(
        on_device,
        mesh=mesh,
        in_specs=(
            P("grp", None, "fsdp"),
            P("fsdp"),
            P(),
            P(),
            P("tp", "fsdp"),
            P(("tp", "fsdp"), None),
            P(),
            P("fsdp", "tp"),
            P(("fsdp", "tp"), None),
            P(),
            P(("grp", "fsdp")),
            P(("grp", "fsdp"), None, "tp", None),
            P(("grp", "fsdp"), None, "tp", None),
        ),
        out_specs=P("grp", None, "fsdp"),
        check_vma=False,
    )
```

```python
import functools
import math

import jax
import jax.numpy as jnp
from jax import lax
from jax.experimental import pallas as pl
from jax.experimental.pallas import tpu as pltpu
from jax.sharding import PartitionSpec as P

D = 5120
BLOCK = 128


epsilon = 1e-06
rope_base = 1000000.0


def head_norm(values, gain):
    return values * lax.rsqrt(jnp.mean(values * values, axis=-1, keepdims=True) + epsilon) * gain


def rotate(values, positions):
    half_dim = values.shape[-1] // 2
    frequency = jnp.exp(
        jnp.arange(half_dim).astype(jnp.float32) * (-2.0 * math.log(rope_base) / values.shape[-1])
    )
    angles = positions.astype(jnp.float32)[..., None] * frequency
    angles = angles.reshape(
        positions.shape + (1,) * (values.ndim - positions.ndim - 1) + (half_dim,)
    )
    cosine = jnp.cos(angles)
    sine_part = jnp.sin(angles)
    first_part = values[..., :half_dim]
    second_part = values[..., half_dim:]
    return jnp.concatenate(
        [
            first_part * cosine - second_part * sine_part,
            second_part * cosine + first_part * sine_part,
        ],
        axis=-1,
    )


def attend(projected, lengths, key_cache, value_cache, q_gain, k_gain):
    row_count = projected.shape[0]
    groups = key_cache.shape[2]
    head_dim = key_cache.shape[3]
    grouped = projected.reshape(row_count, 2, groups, -1, head_dim)
    per_group = grouped.shape[3]
    queries = grouped[:, :, :, : per_group - 2]
    new_keys = grouped[:, :, :, per_group - 2]
    new_values = grouped[:, :, :, per_group - 1].astype(jnp.bfloat16)
    positions = lengths[:, None] + jnp.arange(2, dtype=jnp.int32)[None, :]
    queries = rotate(head_norm(queries, q_gain), positions).astype(jnp.bfloat16)
    new_keys = rotate(head_norm(new_keys, k_gain), positions).astype(jnp.bfloat16)
    scaling = 1.0 / math.sqrt(head_dim)
    cache_scores = (
        jnp.einsum("rsgqd,rlgd->rsgql", queries, key_cache, preferred_element_type=jnp.float32)
        * scaling
    )
    new_scores = (
        jnp.einsum("rsgqd,rtgd->rsgqt", queries, new_keys, preferred_element_type=jnp.float32)
        * scaling
    )
    cache_mask = (
        jnp.arange(key_cache.shape[1], dtype=jnp.int32)[None, :] < lengths[:, None]
    ).reshape(row_count, 1, 1, 1, -1)
    step_mask = (
        jnp.arange(2, dtype=jnp.int32)[None, :] <= jnp.arange(2, dtype=jnp.int32)[:, None]
    ).reshape(1, 2, 1, 1, 2)
    cache_weights = jnp.where(cache_mask, jnp.exp(cache_scores), 0.0)
    new_weights = jnp.where(step_mask, jnp.exp(new_scores), 0.0)
    totals = jnp.sum(cache_weights, axis=-1) + jnp.sum(new_weights, axis=-1)
    cache_weights = (cache_weights / totals[..., None]).astype(jnp.bfloat16)
    new_weights = (new_weights / totals[..., None]).astype(jnp.bfloat16)
    mixed = jnp.einsum(
        "rsgql,rlgd->rsgqd", cache_weights, value_cache, preferred_element_type=jnp.float32
    )
    mixed = mixed + jnp.einsum(
        "rsgqt,rtgd->rsgqd", new_weights, new_values, preferred_element_type=jnp.float32
    )
    return mixed.reshape(row_count, 2, -1).astype(jnp.bfloat16)


MESH = pl.DeviceIdType.MESH
ANY = pl.BlockSpec(memory_space=pl.ANY)


def greet(axes):
    barrier = pltpu.get_barrier_semaphore()
    total = 0
    for axis in axes:
        size = lax.axis_size(axis)
        me = lax.axis_index(axis)
        for step in range(1, size):
            pl.semaphore_signal(
                barrier, inc=1, device_id={axis: lax.rem(me + step, size)}, device_id_type=MESH
            )
        total += size - 1
    pl.semaphore_wait(barrier, total)


def columns_at(index, width):
    start = index * width
    return pl.ds(pl.multiple_of(start, 128) if width % 128 == 0 else start, width)


def landing(ref, split, rows, index, width):
    if split:
        return ref.at[index, rows]
    return ref.at[rows, columns_at(index, width)]


def folds(shards):
    inner = 2 if shards % 2 == 0 else 1
    return shards // inner, inner


def send(source, target, s_sem, r_sem, device):
    copy = pltpu.make_async_remote_copy(
        src_ref=source, dst_ref=target, send_sem=s_sem, recv_sem=r_sem,
        device_id=device, device_id_type=MESH,
    )
    copy.start()
    return copy


class Spread:
    def __init__(self, own, place, sems, over_tp):
        self.own, self.place, self.over_tp = own, place, over_tp
        self.s_sem, self.r_sem, self.s_tp, self.r_tp = sems
        self.shards = lax.axis_size("fsdp")
        self.outer, self.inner = folds(self.shards)
        fsdp = lax.axis_index("fsdp")
        self.hi, self.lo = fsdp // self.inner, lax.rem(fsdp, self.inner)
        self.arriving = {}
        self.sent = []

    def begin(self):
        fsdp = lax.axis_index("fsdp")
        for a in range(1, self.outer):
            at = a * self.inner
            peer = lax.rem(self.hi + a, self.outer) * self.inner + self.lo
            self.arriving[a, 0] = send(
                self.own, self.place(fsdp), self.s_sem.at[at], self.r_sem.at[at], {"fsdp": peer}
            )
        self.inward(0, self.own)

    def inward(self, a, block):
        source_hi = lax.rem(self.hi + self.outer - a, self.outer)
        for b in range(1, self.inner):
            at = a * self.inner + b
            peer = self.hi * self.inner + lax.rem(self.lo + b, self.inner)
            self.arriving[a, b] = send(
                block, self.place(source_hi * self.inner + self.lo),
                self.s_sem.at[at], self.r_sem.at[at], {"fsdp": peer},
            )

    def across(self, a, b):
        if not self.over_tp:
            return
        halves = lax.axis_size("tp")
        tp = lax.axis_index("tp")
        source = lax.rem(self.hi + self.outer - a, self.outer) * self.inner + lax.rem(
            self.lo + self.inner - b, self.inner
        )
        block = self.place(source)
        for c in range(1, halves):
            at = (a * self.inner + b, c)
            self.sent.append(
                send(block, block, self.s_tp.at[at], self.r_tp.at[at], {"tp": lax.rem(tp + c, halves)})
            )

    def pass_on(self):
        for a in range(1, self.outer):
            self.arriving[a, 0].wait_recv()
            source = lax.rem(self.hi + self.outer - a, self.outer) * self.inner + self.lo
            self.inward(a, self.place(source))
            self.across(a, 0)
        for a in range(self.outer):
            for b in range(1, self.inner):
                self.arriving[a, b].wait_recv()
                self.across(a, b)

    def end(self):
        for copy in self.arriving.values():
            copy.wait_send()
        for copy in self.sent:
            copy.wait()


def chunks_of(rows):
    return 2 if rows % 32 == 0 else 1


def relay_kernel(
    split, base, codes, hidden, gain, got_base, got_codes, got_hidden, got_gain,
    s_base, r_base, s_fwd, r_fwd, s_code, r_code, s_hid, r_hid, s_htp, r_htp, s_gain, r_gain, s_local,
):
    groups, shards, halves = lax.axis_size("grp"), lax.axis_size("fsdp"), lax.axis_size("tp")
    grp, fsdp, tp = lax.axis_index("grp"), lax.axis_index("fsdp"), lax.axis_index("tp")
    width = base.shape[1]
    rows = base.shape[0] // shards
    part = rows // groups
    chunks = chunks_of(part)
    size = part // chunks
    code_rows = codes.shape[0]
    code_width = codes.shape[1] // halves
    hidden_part = hidden.shape[0] // halves
    outer, inner = folds(shards)
    greet(("grp", "fsdp", "tp"))

    hidden_rows = pl.ds(pl.multiple_of(tp * hidden_part, 16), hidden_part)
    spread = Spread(
        hidden.at[hidden_rows],
        lambda source: landing(got_hidden, split, hidden_rows, source, width),
        (s_hid, r_hid, s_htp, r_htp),
        True,
    )
    spread.begin()

    def my_rows(chunk, first):
        return pl.ds(pl.multiple_of(first + grp * part + chunk * size, 16), size)

    started = []
    base_copies = []
    hi, lo = fsdp // inner, lax.rem(fsdp, inner)
    for a in range(outer):
        for b in range(inner):
            if a == 0 and b == 0:
                continue
            peer = lax.rem(hi + a, outer) * inner + lax.rem(lo + b, inner)
            source = lax.rem(hi + outer - a, outer) * inner + lax.rem(lo + inner - b, inner)
            step = a * inner + b
            started.append(
                send(
                    gain, got_gain.at[fsdp], s_gain.at[step], r_gain.at[step], {"fsdp": peer}
                )
            )
            for chunk in range(chunks):
                at = (step, chunk)
                copy = send(
                    base.at[my_rows(chunk, peer * rows)],
                    landing(got_base, split, my_rows(chunk, 0), fsdp, width),
                    s_base.at[at], r_base.at[at], {"fsdp": peer},
                )
                base_copies.append((copy, step, chunk, source))
    own_rows = pl.ds(pl.multiple_of(tp * code_rows, 16), code_rows)
    for step in range(1, halves):
        peer = lax.rem(tp + step, halves)
        started.append(
            send(
                codes.at[:, columns_at(peer, code_width)], got_codes.at[own_rows],
                s_code.at[step], r_code.at[step], {"tp": peer},
            )
        )
    local = [
        pltpu.make_async_copy(
            codes.at[:, columns_at(tp, code_width)], got_codes.at[own_rows], s_local.at[0]
        ),
        pltpu.make_async_copy(
            base.at[pl.ds(pl.multiple_of(fsdp * rows, 16), rows)],
            landing(got_base, split, pl.ds(0, rows), fsdp, width),
            s_local.at[1],
        ),
        pltpu.make_async_copy(
            hidden, landing(got_hidden, split, pl.ds(0, hidden.shape[0]), fsdp, width), s_local.at[2]
        ),
        pltpu.make_async_copy(gain, got_gain.at[fsdp], s_local.at[3]),
    ]
    for copy in local:
        copy.start()
    spread.pass_on()
    for copy, step, chunk, source in base_copies:
        copy.wait_recv()
        block = landing(got_base, split, my_rows(chunk, 0), source, width)
        for hop in range(1, groups):
            at = (step * chunks + chunk, hop)
            started.append(
                send(
                    block, block, s_fwd.at[at], r_fwd.at[at], {"grp": lax.rem(grp + hop, groups)}
                )
            )
    spread.end()
    for copy, _, _, _ in base_copies:
        copy.wait_send()
    for copy in started:
        copy.wait()
    for copy in local:
        copy.wait()


def relay(base, codes, hidden, gain, grp_size, shards, halves):
    width = base.shape[1]
    rows = base.shape[0] // shards
    chunks = chunks_of(rows // grp_size)
    split = width % 128 != 0

    def gathered(count):
        return (shards, count, width) if split else (count, shards * width)

    dma = pltpu.SemaphoreType.DMA
    got_base, got_codes, got_hidden, got_gain = pl.pallas_call(
        functools.partial(relay_kernel, split),
        out_shape=(
            jax.ShapeDtypeStruct(gathered(rows), base.dtype),
            jax.ShapeDtypeStruct((codes.shape[0] * halves, codes.shape[1] // halves), codes.dtype),
            jax.ShapeDtypeStruct(gathered(hidden.shape[0]), hidden.dtype),
            jax.ShapeDtypeStruct((shards, 8, width), gain.dtype),
        ),
        in_specs=[ANY] * 4,
        out_specs=(ANY,) * 4,
        scratch_shapes=[
            dma((shards, chunks)), dma((shards, chunks)),
            dma((shards * chunks, grp_size)), dma((shards * chunks, grp_size)),
            dma((halves,)), dma((halves,)),
            dma((shards,)), dma((shards,)), dma((shards, halves)), dma((shards, halves)),
            dma((shards,)), dma((shards,)), dma((4,)),
        ],
        compiler_params=pltpu.CompilerParams(collective_id=0, has_side_effects=True),
        cost_estimate=pl.CostEstimate(flops=0, bytes_accessed=250_000_000, transcendentals=0),
        name="relay",
    )(base, codes, hidden, jnp.broadcast_to(gain[None], (8, width)))
    if split:
        got_base = jnp.swapaxes(got_base, 0, 1).reshape(rows, shards * width)
        got_hidden = jnp.swapaxes(got_hidden, 0, 1).reshape(-1, shards * width)
    return got_base, got_codes, got_hidden, got_gain[:, 0].reshape(-1)


def gather_kernel(values, got, s_sem, r_sem, s_local):
    rows = values.shape[0]
    greet(("fsdp",))

    def place(source):
        return got.at[pl.ds(pl.multiple_of(source * rows, 16), rows)]

    spread = Spread(values, place, (s_sem, r_sem, None, None), False)
    spread.begin()
    local = pltpu.make_async_copy(values, place(lax.axis_index("fsdp")), s_local)
    local.start()
    spread.pass_on()
    spread.end()
    local.wait()


def gather_rows(values, shards):
    dma = pltpu.SemaphoreType.DMA
    return pl.pallas_call(
        gather_kernel,
        out_shape=jax.ShapeDtypeStruct((values.shape[0] * shards, values.shape[1]), values.dtype),
        in_specs=[ANY],
        out_specs=ANY,
        scratch_shapes=[dma((shards,)), dma((shards,)), dma],
        compiler_params=pltpu.CompilerParams(collective_id=2, has_side_effects=True),
        name="gather_rows",
    )(values)


def to_rows_kernel(split, values, got, s_sem, r_sem, s_local):
    shards = lax.axis_size("fsdp")
    fsdp = lax.axis_index("fsdp")
    rows = values.shape[0] // shards
    width = values.shape[1]
    greet(("fsdp",))
    every = pl.ds(0, rows)
    copies = []
    for step in range(1, shards):
        peer = lax.rem(fsdp + step, shards)
        copy = pltpu.make_async_remote_copy(
            src_ref=values.at[pl.ds(pl.multiple_of(peer * rows, 8), rows)],
            dst_ref=landing(got, split, every, fsdp, width),
            send_sem=s_sem.at[step],
            recv_sem=r_sem.at[step],
            device_id={"fsdp": peer},
            device_id_type=MESH,
        )
        copy.start()
        copies.append(copy)
    local = pltpu.make_async_copy(
        values.at[pl.ds(pl.multiple_of(fsdp * rows, 8), rows)],
        landing(got, split, every, fsdp, width),
        s_local,
    )
    local.start()
    for copy in copies:
        copy.wait()
    local.wait()


def to_rows(values, shards):
    rows = values.shape[0] // shards
    width = values.shape[1]
    split = width % 128 != 0
    dma = pltpu.SemaphoreType.DMA
    got = pl.pallas_call(
        functools.partial(to_rows_kernel, split),
        out_shape=jax.ShapeDtypeStruct(
            (shards, rows, width) if split else (rows, shards * width), values.dtype
        ),
        in_specs=[ANY],
        out_specs=ANY,
        scratch_shapes=[dma((shards,)), dma((shards,)), dma],
        compiler_params=pltpu.CompilerParams(collective_id=1, has_side_effects=True),
        name="to_rows",
    )(values)
    if split:
        got = jnp.swapaxes(got, 0, 1).reshape(rows, shards * width)
    return got


def updated_matmul_kernel(x, base, codes, scale, out):
    depth = x.shape[1]

    @pl.when(pl.program_id(0) == 0)
    def _():
        out[...] = jnp.zeros_like(out)

    parts = []
    for block in range(depth // BLOCK):
        at = slice(block * BLOCK, (block + 1) * BLOCK)
        delta = codes[:, at].astype(jnp.float32) * scale[0, :, block : block + 1]
        parts.append((base[:, at].astype(jnp.float32) + delta).astype(jnp.bfloat16))
    out[...] += lax.dot_general(
        x[...], jnp.concatenate(parts, axis=1), (((1,), (1,)), ((), ())),
        preferred_element_type=jnp.float32,
    )


def updated_matmul(x, base, codes, row_scale, depth=512):
    count, total = base.shape
    steps = total // depth
    scale = row_scale.reshape(count, steps, depth // BLOCK).transpose(1, 0, 2)
    return pl.pallas_call(
        updated_matmul_kernel,
        grid=(steps,),
        out_shape=jax.ShapeDtypeStruct((x.shape[0], count), jnp.float32),
        in_specs=[
            pl.BlockSpec((x.shape[0], depth), lambda i: (0, i)),
            pl.BlockSpec((count, depth), lambda i: (0, i)),
            pl.BlockSpec((count, depth), lambda i: (0, i)),
            pl.BlockSpec((1, count, depth // BLOCK), lambda i: (i, 0, 0)),
        ],
        out_specs=pl.BlockSpec((x.shape[0], count), lambda i: (0, 0)),
        compiler_params=pltpu.CompilerParams(vmem_limit_bytes=56 * 2**20),
        cost_estimate=pl.CostEstimate(
            flops=2 * x.shape[0] * count * total, bytes_accessed=4 * count * total, transcendentals=0
        ),
        name="updated_matmul",
    )(x, base, codes, scale)


def row_scales(scale, first_row, rows):
    ids = (first_row + jnp.arange(rows, dtype=jnp.int32)) // BLOCK
    pick = (ids[:, None] == jnp.arange(scale.shape[0], dtype=jnp.int32)[None, :]).astype(jnp.float32)
    return jnp.dot(pick, scale, precision=lax.Precision.HIGHEST)


def on_device(
    hidden,
    input_gain,
    q_gain,
    k_gain,
    base_qkv,
    codes_qkv,
    scale_qkv,
    base_out,
    codes_out,
    scale_out,
    lengths,
    key_cache,
    value_cache,
):
    grp_size, shards, halves = lax.axis_size("grp"), lax.axis_size("fsdp"), lax.axis_size("tp")
    fsdp_index = lax.axis_index("fsdp")
    tp_index = lax.axis_index("tp")
    row_count = hidden.shape[0]
    arrived_base, arrived_out, whole_hidden, whole_gain = relay(
        base_qkv, codes_out, hidden.reshape(row_count * 2, -1), input_gain, grp_size, shards, halves
    )

    hidden_float = whole_hidden.astype(jnp.float32)
    mean_square = jnp.sum(hidden_float * hidden_float, axis=-1) / D
    normed = (hidden_float * lax.rsqrt(mean_square + epsilon)[..., None] * whole_gain).astype(
        jnp.bfloat16
    )
    qkv_rows = codes_qkv.shape[0]
    qkv_scale = row_scales(scale_qkv, (tp_index * shards + fsdp_index) * qkv_rows, qkv_rows)
    projected = updated_matmul(normed, arrived_base, codes_qkv, qkv_scale)
    projected = to_rows(projected, shards).reshape(row_count // shards, 2, -1)
    attended = attend(projected, lengths, key_cache, value_cache, q_gain, k_gain)

    out_rows, out_columns = base_out.shape
    column_blocks = out_columns // BLOCK
    scale_columns = lax.dynamic_slice_in_dim(scale_out, tp_index * column_blocks, column_blocks, 1)
    out_scale = row_scales(scale_columns, fsdp_index * out_rows, out_rows)
    whole_attended = gather_rows(attended.reshape(-1, attended.shape[-1]), shards)
    partial_out = updated_matmul(whole_attended, base_out, arrived_out, out_scale)
    return lax.psum(partial_out, "tp").astype(jnp.bfloat16).reshape(row_count, 2, out_rows)


def solution(mesh):
    return jax.shard_map(
        on_device,
        mesh=mesh,
        in_specs=(
            P("grp", None, "fsdp"),
            P("fsdp"),
            P(),
            P(),
            P("tp", "fsdp"),
            P(("tp", "fsdp"), None),
            P(),
            P("fsdp", "tp"),
            P(("fsdp", "tp"), None),
            P(),
            P(("grp", "fsdp")),
            P(("grp", "fsdp"), None, "tp", None),
            P(("grp", "fsdp"), None, "tp", None),
        ),
        out_specs=P("grp", None, "fsdp"),
        check_vma=False,
    )
```

```python
import functools
import math

import jax
import jax.numpy as jnp
from jax import lax
from jax.experimental import pallas as pl
from jax.experimental.pallas import tpu as pltpu
from jax.sharding import PartitionSpec as P

D = 5120
BLOCK = 128


epsilon = 1e-06
rope_base = 1000000.0


def head_norm(values, gain):
    return values * lax.rsqrt(jnp.mean(values * values, axis=-1, keepdims=True) + epsilon) * gain


def rotate(values, positions):
    half_dim = values.shape[-1] // 2
    frequency = jnp.exp(
        jnp.arange(half_dim).astype(jnp.float32) * (-2.0 * math.log(rope_base) / values.shape[-1])
    )
    angles = positions.astype(jnp.float32)[..., None] * frequency
    angles = angles.reshape(
        positions.shape + (1,) * (values.ndim - positions.ndim - 1) + (half_dim,)
    )
    cosine = jnp.cos(angles)
    sine_part = jnp.sin(angles)
    first_part = values[..., :half_dim]
    second_part = values[..., half_dim:]
    return jnp.concatenate(
        [
            first_part * cosine - second_part * sine_part,
            second_part * cosine + first_part * sine_part,
        ],
        axis=-1,
    )


def attend(projected, lengths, key_cache, value_cache, q_gain, k_gain):
    row_count = projected.shape[0]
    groups = key_cache.shape[2]
    head_dim = key_cache.shape[3]
    grouped = projected.reshape(row_count, 2, groups, -1, head_dim)
    per_group = grouped.shape[3]
    queries = grouped[:, :, :, : per_group - 2]
    new_keys = grouped[:, :, :, per_group - 2]
    new_values = grouped[:, :, :, per_group - 1].astype(jnp.bfloat16)
    positions = lengths[:, None] + jnp.arange(2, dtype=jnp.int32)[None, :]
    queries = rotate(head_norm(queries, q_gain), positions).astype(jnp.bfloat16)
    new_keys = rotate(head_norm(new_keys, k_gain), positions).astype(jnp.bfloat16)
    scaling = 1.0 / math.sqrt(head_dim)
    cache_scores = (
        jnp.einsum("rsgqd,rlgd->rsgql", queries, key_cache, preferred_element_type=jnp.float32)
        * scaling
    )
    new_scores = (
        jnp.einsum("rsgqd,rtgd->rsgqt", queries, new_keys, preferred_element_type=jnp.float32)
        * scaling
    )
    cache_mask = (
        jnp.arange(key_cache.shape[1], dtype=jnp.int32)[None, :] < lengths[:, None]
    ).reshape(row_count, 1, 1, 1, -1)
    step_mask = (
        jnp.arange(2, dtype=jnp.int32)[None, :] <= jnp.arange(2, dtype=jnp.int32)[:, None]
    ).reshape(1, 2, 1, 1, 2)
    cache_weights = jnp.where(cache_mask, jnp.exp(cache_scores), 0.0)
    new_weights = jnp.where(step_mask, jnp.exp(new_scores), 0.0)
    totals = jnp.sum(cache_weights, axis=-1) + jnp.sum(new_weights, axis=-1)
    cache_weights = (cache_weights / totals[..., None]).astype(jnp.bfloat16)
    new_weights = (new_weights / totals[..., None]).astype(jnp.bfloat16)
    mixed = jnp.einsum(
        "rsgql,rlgd->rsgqd", cache_weights, value_cache, preferred_element_type=jnp.float32
    )
    mixed = mixed + jnp.einsum(
        "rsgqt,rtgd->rsgqd", new_weights, new_values, preferred_element_type=jnp.float32
    )
    return mixed.reshape(row_count, 2, -1).astype(jnp.bfloat16)


MESH = pl.DeviceIdType.MESH
ANY = pl.BlockSpec(memory_space=pl.ANY)


def greet(axes):
    barrier = pltpu.get_barrier_semaphore()
    total = 0
    for axis in axes:
        size = lax.axis_size(axis)
        me = lax.axis_index(axis)
        for step in range(1, size):
            pl.semaphore_signal(
                barrier, inc=1, device_id={axis: lax.rem(me + step, size)}, device_id_type=MESH
            )
        total += size - 1
    pl.semaphore_wait(barrier, total)


def columns_at(index, width):
    start = index * width
    return pl.ds(pl.multiple_of(start, 128) if width % 128 == 0 else start, width)


def landing(ref, split, rows, index, width):
    if split:
        return ref.at[index, rows]
    return ref.at[rows, columns_at(index, width)]


def folds(shards):
    inner = 2 if shards % 2 == 0 else 1
    return shards // inner, inner


def send(source, target, s_sem, r_sem, device):
    copy = pltpu.make_async_remote_copy(
        src_ref=source, dst_ref=target, send_sem=s_sem, recv_sem=r_sem,
        device_id=device, device_id_type=MESH,
    )
    copy.start()
    return copy


class Spread:
    def __init__(self, own, place, sems, over_tp):
        self.own, self.place, self.over_tp = own, place, over_tp
        self.s_sem, self.r_sem, self.s_tp, self.r_tp = sems
        self.shards = lax.axis_size("fsdp")
        self.outer, self.inner = folds(self.shards)
        fsdp = lax.axis_index("fsdp")
        self.hi, self.lo = fsdp // self.inner, lax.rem(fsdp, self.inner)
        self.arriving = {}
        self.sent = []

    def begin(self):
        fsdp = lax.axis_index("fsdp")
        for a in range(1, self.outer):
            at = a * self.inner
            peer = lax.rem(self.hi + a, self.outer) * self.inner + self.lo
            self.arriving[a, 0] = send(
                self.own, self.place(fsdp), self.s_sem.at[at], self.r_sem.at[at], {"fsdp": peer}
            )
        self.inward(0, self.own)

    def inward(self, a, block):
        source_hi = lax.rem(self.hi + self.outer - a, self.outer)
        for b in range(1, self.inner):
            at = a * self.inner + b
            peer = self.hi * self.inner + lax.rem(self.lo + b, self.inner)
            self.arriving[a, b] = send(
                block, self.place(source_hi * self.inner + self.lo),
                self.s_sem.at[at], self.r_sem.at[at], {"fsdp": peer},
            )

    def across(self, a, b):
        if not self.over_tp:
            return
        halves = lax.axis_size("tp")
        tp = lax.axis_index("tp")
        source = lax.rem(self.hi + self.outer - a, self.outer) * self.inner + lax.rem(
            self.lo + self.inner - b, self.inner
        )
        block = self.place(source)
        for c in range(1, halves):
            at = (a * self.inner + b, c)
            self.sent.append(
                send(block, block, self.s_tp.at[at], self.r_tp.at[at], {"tp": lax.rem(tp + c, halves)})
            )

    def pass_on(self):
        for a in range(1, self.outer):
            self.arriving[a, 0].wait_recv()
            source = lax.rem(self.hi + self.outer - a, self.outer) * self.inner + self.lo
            self.inward(a, self.place(source))
            self.across(a, 0)
        for a in range(self.outer):
            for b in range(1, self.inner):
                self.arriving[a, b].wait_recv()
                self.across(a, b)

    def end(self):
        for copy in self.arriving.values():
            copy.wait_send()
        for copy in self.sent:
            copy.wait()


def chunks_of(rows):
    return 4 if rows % 64 == 0 else 2 if rows % 32 == 0 else 1


WINDOW = 6


def relay_kernel(
    split, base, codes, hidden, gain, got_base, got_codes, got_hidden, got_gain,
    s_base, r_base, s_fwd, r_fwd, s_code, r_code, s_hid, r_hid, s_htp, r_htp, s_gain, r_gain, s_local,
):
    groups, shards, halves = lax.axis_size("grp"), lax.axis_size("fsdp"), lax.axis_size("tp")
    grp, fsdp, tp = lax.axis_index("grp"), lax.axis_index("fsdp"), lax.axis_index("tp")
    width = base.shape[1]
    rows = base.shape[0] // shards
    part = rows // groups
    chunks = chunks_of(part)
    size = part // chunks
    code_rows = codes.shape[0]
    code_width = codes.shape[1] // halves
    hidden_part = hidden.shape[0] // halves
    outer, inner = folds(shards)
    greet(("grp", "fsdp", "tp"))

    hidden_rows = pl.ds(pl.multiple_of(tp * hidden_part, 16), hidden_part)
    spread = Spread(
        hidden.at[hidden_rows],
        lambda source: landing(got_hidden, split, hidden_rows, source, width),
        (s_hid, r_hid, s_htp, r_htp),
        True,
    )
    spread.begin()

    def my_rows(chunk, first):
        return pl.ds(pl.multiple_of(first + grp * part + chunk * size, 16), size)

    started = []
    plan = []
    hi, lo = fsdp // inner, lax.rem(fsdp, inner)
    for a in range(outer):
        for b in range(inner):
            if a == 0 and b == 0:
                continue
            peer = lax.rem(hi + a, outer) * inner + lax.rem(lo + b, inner)
            source = lax.rem(hi + outer - a, outer) * inner + lax.rem(lo + inner - b, inner)
            step = a * inner + b
            started.append(
                send(
                    gain, got_gain.at[fsdp], s_gain.at[step], r_gain.at[step], {"fsdp": peer}
                )
            )
            plan += [(step, chunk, peer, source) for chunk in range(chunks)]

    def send_base(step, chunk, peer, source):
        at = (step, chunk)
        return send(
            base.at[my_rows(chunk, peer * rows)],
            landing(got_base, split, my_rows(chunk, 0), fsdp, width),
            s_base.at[at], r_base.at[at], {"fsdp": peer},
        )

    flying = [send_base(*entry) for entry in plan[:WINDOW]]
    own_rows = pl.ds(pl.multiple_of(tp * code_rows, 16), code_rows)
    for step in range(1, halves):
        peer = lax.rem(tp + step, halves)
        started.append(
            send(
                codes.at[:, columns_at(peer, code_width)], got_codes.at[own_rows],
                s_code.at[step], r_code.at[step], {"tp": peer},
            )
        )
    local = [
        pltpu.make_async_copy(
            codes.at[:, columns_at(tp, code_width)], got_codes.at[own_rows], s_local.at[0]
        ),
        pltpu.make_async_copy(
            base.at[pl.ds(pl.multiple_of(fsdp * rows, 16), rows)],
            landing(got_base, split, pl.ds(0, rows), fsdp, width),
            s_local.at[1],
        ),
        pltpu.make_async_copy(
            hidden, landing(got_hidden, split, pl.ds(0, hidden.shape[0]), fsdp, width), s_local.at[2]
        ),
        pltpu.make_async_copy(gain, got_gain.at[fsdp], s_local.at[3]),
    ]
    for copy in local:
        copy.start()
    spread.pass_on()
    for index, (step, chunk, _, source) in enumerate(plan):
        copy = flying[index]
        copy.wait_send()
        if index + WINDOW < len(plan):
            flying.append(send_base(*plan[index + WINDOW]))
        copy.wait_recv()
        block = landing(got_base, split, my_rows(chunk, 0), source, width)
        for hop in range(1, groups):
            at = (step * chunks + chunk, hop)
            started.append(
                send(
                    block, block, s_fwd.at[at], r_fwd.at[at], {"grp": lax.rem(grp + hop, groups)}
                )
            )
    spread.end()
    for copy in started:
        copy.wait()
    for copy in local:
        copy.wait()


def relay(base, codes, hidden, gain, grp_size, shards, halves):
    width = base.shape[1]
    rows = base.shape[0] // shards
    chunks = chunks_of(rows // grp_size)
    split = width % 128 != 0

    def gathered(count):
        return (shards, count, width) if split else (count, shards * width)

    dma = pltpu.SemaphoreType.DMA
    got_base, got_codes, got_hidden, got_gain = pl.pallas_call(
        functools.partial(relay_kernel, split),
        out_shape=(
            jax.ShapeDtypeStruct(gathered(rows), base.dtype),
            jax.ShapeDtypeStruct((codes.shape[0] * halves, codes.shape[1] // halves), codes.dtype),
            jax.ShapeDtypeStruct(gathered(hidden.shape[0]), hidden.dtype),
            jax.ShapeDtypeStruct((shards, 1, width), gain.dtype),
        ),
        in_specs=[ANY] * 4,
        out_specs=(ANY,) * 4,
        scratch_shapes=[
            dma((shards, chunks)), dma((shards, chunks)),
            dma((shards * chunks, grp_size)), dma((shards * chunks, grp_size)),
            dma((halves,)), dma((halves,)),
            dma((shards,)), dma((shards,)), dma((shards, halves)), dma((shards, halves)),
            dma((shards,)), dma((shards,)), dma((4,)),
        ],
        compiler_params=pltpu.CompilerParams(collective_id=0, has_side_effects=True),
        cost_estimate=pl.CostEstimate(flops=0, bytes_accessed=250_000_000, transcendentals=0),
        name="relay",
    )(base, codes, hidden, gain[None])
    if split:
        got_base = jnp.swapaxes(got_base, 0, 1).reshape(rows, shards * width)
        got_hidden = jnp.swapaxes(got_hidden, 0, 1).reshape(-1, shards * width)
    return got_base, got_codes, got_hidden, got_gain.reshape(-1)


def gather_kernel(values, got, s_sem, r_sem, s_local):
    rows = values.shape[0]
    greet(("fsdp",))

    def place(source):
        return got.at[pl.ds(pl.multiple_of(source * rows, 16), rows)]

    spread = Spread(values, place, (s_sem, r_sem, None, None), False)
    spread.begin()
    local = pltpu.make_async_copy(values, place(lax.axis_index("fsdp")), s_local)
    local.start()
    spread.pass_on()
    spread.end()
    local.wait()


def gather_rows(values, shards):
    dma = pltpu.SemaphoreType.DMA
    return pl.pallas_call(
        gather_kernel,
        out_shape=jax.ShapeDtypeStruct((values.shape[0] * shards, values.shape[1]), values.dtype),
        in_specs=[ANY],
        out_specs=ANY,
        scratch_shapes=[dma((shards,)), dma((shards,)), dma],
        compiler_params=pltpu.CompilerParams(collective_id=2, has_side_effects=True),
        name="gather_rows",
    )(values)


def to_rows_kernel(split, values, got, s_sem, r_sem, s_local):
    shards = lax.axis_size("fsdp")
    fsdp = lax.axis_index("fsdp")
    rows = values.shape[0] // shards
    width = values.shape[1]
    greet(("fsdp",))
    every = pl.ds(0, rows)
    copies = []
    for step in range(1, shards):
        peer = lax.rem(fsdp + step, shards)
        copy = pltpu.make_async_remote_copy(
            src_ref=values.at[pl.ds(pl.multiple_of(peer * rows, 8), rows)],
            dst_ref=landing(got, split, every, fsdp, width),
            send_sem=s_sem.at[step],
            recv_sem=r_sem.at[step],
            device_id={"fsdp": peer},
            device_id_type=MESH,
        )
        copy.start()
        copies.append(copy)
    local = pltpu.make_async_copy(
        values.at[pl.ds(pl.multiple_of(fsdp * rows, 8), rows)],
        landing(got, split, every, fsdp, width),
        s_local,
    )
    local.start()
    for copy in copies:
        copy.wait()
    local.wait()


def to_rows(values, shards):
    rows = values.shape[0] // shards
    width = values.shape[1]
    split = width % 128 != 0
    dma = pltpu.SemaphoreType.DMA
    got = pl.pallas_call(
        functools.partial(to_rows_kernel, split),
        out_shape=jax.ShapeDtypeStruct(
            (shards, rows, width) if split else (rows, shards * width), values.dtype
        ),
        in_specs=[ANY],
        out_specs=ANY,
        scratch_shapes=[dma((shards,)), dma((shards,)), dma],
        compiler_params=pltpu.CompilerParams(collective_id=1, has_side_effects=True),
        name="to_rows",
    )(values)
    if split:
        got = jnp.swapaxes(got, 0, 1).reshape(rows, shards * width)
    return got


def updated_matmul_kernel(x, base, codes, scale, out):
    depth = x.shape[1]

    @pl.when(pl.program_id(0) == 0)
    def _():
        out[...] = jnp.zeros_like(out)

    bands = scale.shape[0]
    height = base.shape[0] // bands
    columns = depth // BLOCK
    first = pl.program_id(0) * columns
    rows = []
    for band in range(bands):
        here = slice(band * height, (band + 1) * height)
        parts = []
        for block in range(columns):
            at = slice(block * BLOCK, (block + 1) * BLOCK)
            delta = codes[here, at].astype(jnp.float32) * scale[band, first + block]
            parts.append((base[here, at].astype(jnp.float32) + delta).astype(jnp.bfloat16))
        rows.append(jnp.concatenate(parts, axis=1))
    out[...] += lax.dot_general(
        x[...], jnp.concatenate(rows, axis=0), (((1,), (1,)), ((), ())),
        preferred_element_type=jnp.float32,
    )


def updated_matmul(x, base, codes, band_scale, depth=512):
    count, total = base.shape
    steps = total // depth
    return pl.pallas_call(
        updated_matmul_kernel,
        grid=(steps,),
        out_shape=jax.ShapeDtypeStruct((x.shape[0], count), jnp.float32),
        in_specs=[
            pl.BlockSpec((x.shape[0], depth), lambda i: (0, i)),
            pl.BlockSpec((count, depth), lambda i: (0, i)),
            pl.BlockSpec((count, depth), lambda i: (0, i)),
            pl.BlockSpec(memory_space=pltpu.SMEM),
        ],
        out_specs=pl.BlockSpec((x.shape[0], count), lambda i: (0, 0)),
        compiler_params=pltpu.CompilerParams(vmem_limit_bytes=56 * 2**20),
        cost_estimate=pl.CostEstimate(
            flops=2 * x.shape[0] * count * total, bytes_accessed=4 * count * total, transcendentals=0
        ),
        name="updated_matmul",
    )(x, base, codes, band_scale)


def band_scales(scale, first_row, rows):
    height = math.gcd(rows, BLOCK)
    ids = (first_row + height * jnp.arange(rows // height, dtype=jnp.int32)) // BLOCK
    pick = (ids[:, None] == jnp.arange(scale.shape[0], dtype=jnp.int32)[None, :]).astype(jnp.float32)
    return jnp.dot(pick, scale, precision=lax.Precision.HIGHEST)


def on_device(
    hidden,
    input_gain,
    q_gain,
    k_gain,
    base_qkv,
    codes_qkv,
    scale_qkv,
    base_out,
    codes_out,
    scale_out,
    lengths,
    key_cache,
    value_cache,
):
    grp_size, shards, halves = lax.axis_size("grp"), lax.axis_size("fsdp"), lax.axis_size("tp")
    fsdp_index = lax.axis_index("fsdp")
    tp_index = lax.axis_index("tp")
    row_count = hidden.shape[0]
    arrived_base, arrived_out, whole_hidden, whole_gain = relay(
        base_qkv, codes_out, hidden.reshape(row_count * 2, -1), input_gain, grp_size, shards, halves
    )

    hidden_float = whole_hidden.astype(jnp.float32)
    mean_square = jnp.sum(hidden_float * hidden_float, axis=-1) / D
    normed = (hidden_float * lax.rsqrt(mean_square + epsilon)[..., None] * whole_gain).astype(
        jnp.bfloat16
    )
    qkv_rows = codes_qkv.shape[0]
    qkv_scale = band_scales(scale_qkv, (tp_index * shards + fsdp_index) * qkv_rows, qkv_rows)
    projected = updated_matmul(normed, arrived_base, codes_qkv, qkv_scale)
    projected = to_rows(projected, shards).reshape(row_count // shards, 2, -1)
    attended = attend(projected, lengths, key_cache, value_cache, q_gain, k_gain)

    out_rows, out_columns = base_out.shape
    column_blocks = out_columns // BLOCK
    scale_columns = lax.dynamic_slice_in_dim(scale_out, tp_index * column_blocks, column_blocks, 1)
    out_scale = band_scales(scale_columns, fsdp_index * out_rows, out_rows)
    whole_attended = gather_rows(attended.reshape(-1, attended.shape[-1]), shards)
    partial_out = updated_matmul(whole_attended, base_out, arrived_out, out_scale)
    return lax.psum(partial_out, "tp").astype(jnp.bfloat16).reshape(row_count, 2, out_rows)


def solution(mesh):
    return jax.shard_map(
        on_device,
        mesh=mesh,
        in_specs=(
            P("grp", None, "fsdp"),
            P("fsdp"),
            P(),
            P(),
            P("tp", "fsdp"),
            P(("tp", "fsdp"), None),
            P(),
            P("fsdp", "tp"),
            P(("fsdp", "tp"), None),
            P(),
            P(("grp", "fsdp")),
            P(("grp", "fsdp"), None, "tp", None),
            P(("grp", "fsdp"), None, "tp", None),
        ),
        out_specs=P("grp", None, "fsdp"),
        check_vma=False,
    )
```

```python
import functools
import math

import jax
import jax.numpy as jnp
from jax import lax
from jax.experimental import pallas as pl
from jax.experimental.pallas import tpu as pltpu
from jax.sharding import PartitionSpec as P

D = 5120
BLOCK = 128


epsilon = 1e-06
rope_base = 1000000.0


def head_norm(values, gain):
    return values * lax.rsqrt(jnp.mean(values * values, axis=-1, keepdims=True) + epsilon) * gain


def rotate(values, positions):
    half_dim = values.shape[-1] // 2
    frequency = jnp.exp(
        jnp.arange(half_dim).astype(jnp.float32) * (-2.0 * math.log(rope_base) / values.shape[-1])
    )
    angles = positions.astype(jnp.float32)[..., None] * frequency
    angles = angles.reshape(
        positions.shape + (1,) * (values.ndim - positions.ndim - 1) + (half_dim,)
    )
    cosine = jnp.cos(angles)
    sine_part = jnp.sin(angles)
    first_part = values[..., :half_dim]
    second_part = values[..., half_dim:]
    return jnp.concatenate(
        [
            first_part * cosine - second_part * sine_part,
            second_part * cosine + first_part * sine_part,
        ],
        axis=-1,
    )


def attend(projected, lengths, key_cache, value_cache, q_gain, k_gain):
    row_count = projected.shape[0]
    groups = key_cache.shape[2]
    head_dim = key_cache.shape[3]
    grouped = projected.reshape(row_count, 2, groups, -1, head_dim)
    per_group = grouped.shape[3]
    queries = grouped[:, :, :, : per_group - 2]
    new_keys = grouped[:, :, :, per_group - 2]
    new_values = grouped[:, :, :, per_group - 1].astype(jnp.bfloat16)
    positions = lengths[:, None] + jnp.arange(2, dtype=jnp.int32)[None, :]
    queries = rotate(head_norm(queries, q_gain), positions).astype(jnp.bfloat16)
    new_keys = rotate(head_norm(new_keys, k_gain), positions).astype(jnp.bfloat16)
    scaling = 1.0 / math.sqrt(head_dim)
    cache_scores = (
        jnp.einsum("rsgqd,rlgd->rsgql", queries, key_cache, preferred_element_type=jnp.float32)
        * scaling
    )
    new_scores = (
        jnp.einsum("rsgqd,rtgd->rsgqt", queries, new_keys, preferred_element_type=jnp.float32)
        * scaling
    )
    cache_mask = (
        jnp.arange(key_cache.shape[1], dtype=jnp.int32)[None, :] < lengths[:, None]
    ).reshape(row_count, 1, 1, 1, -1)
    step_mask = (
        jnp.arange(2, dtype=jnp.int32)[None, :] <= jnp.arange(2, dtype=jnp.int32)[:, None]
    ).reshape(1, 2, 1, 1, 2)
    cache_weights = jnp.where(cache_mask, jnp.exp(cache_scores), 0.0)
    new_weights = jnp.where(step_mask, jnp.exp(new_scores), 0.0)
    totals = jnp.sum(cache_weights, axis=-1) + jnp.sum(new_weights, axis=-1)
    cache_weights = (cache_weights / totals[..., None]).astype(jnp.bfloat16)
    new_weights = (new_weights / totals[..., None]).astype(jnp.bfloat16)
    mixed = jnp.einsum(
        "rsgql,rlgd->rsgqd", cache_weights, value_cache, preferred_element_type=jnp.float32
    )
    mixed = mixed + jnp.einsum(
        "rsgqt,rtgd->rsgqd", new_weights, new_values, preferred_element_type=jnp.float32
    )
    return mixed.reshape(row_count, 2, -1).astype(jnp.bfloat16)


MESH = pl.DeviceIdType.MESH
ANY = pl.BlockSpec(memory_space=pl.ANY)


def greet(axes):
    barrier = pltpu.get_barrier_semaphore()
    total = 0
    for axis in axes:
        size = lax.axis_size(axis)
        me = lax.axis_index(axis)
        for step in range(1, size):
            pl.semaphore_signal(
                barrier, inc=1, device_id={axis: lax.rem(me + step, size)}, device_id_type=MESH
            )
        total += size - 1
    pl.semaphore_wait(barrier, total)


def columns_at(index, width):
    start = index * width
    return pl.ds(pl.multiple_of(start, 128) if width % 128 == 0 else start, width)


def landing(ref, split, rows, index, width):
    if split:
        return ref.at[index, rows]
    return ref.at[rows, columns_at(index, width)]


def folds(shards):
    inner = 2 if shards % 2 == 0 else 1
    return shards // inner, inner


def send(source, target, s_sem, r_sem, device):
    copy = pltpu.make_async_remote_copy(
        src_ref=source, dst_ref=target, send_sem=s_sem, recv_sem=r_sem,
        device_id=device, device_id_type=MESH,
    )
    copy.start()
    return copy


class Spread:
    def __init__(self, own, place, sems, over_tp):
        self.own, self.place, self.over_tp = own, place, over_tp
        self.s_sem, self.r_sem, self.s_tp, self.r_tp = sems
        self.shards = lax.axis_size("fsdp")
        self.outer, self.inner = folds(self.shards)
        fsdp = lax.axis_index("fsdp")
        self.hi, self.lo = fsdp // self.inner, lax.rem(fsdp, self.inner)
        self.arriving = {}
        self.sent = []

    def begin(self):
        fsdp = lax.axis_index("fsdp")
        for a in range(1, self.outer):
            at = a * self.inner
            peer = lax.rem(self.hi + a, self.outer) * self.inner + self.lo
            self.arriving[a, 0] = send(
                self.own, self.place(fsdp), self.s_sem.at[at], self.r_sem.at[at], {"fsdp": peer}
            )
        self.inward(0, self.own)

    def inward(self, a, block):
        source_hi = lax.rem(self.hi + self.outer - a, self.outer)
        for b in range(1, self.inner):
            at = a * self.inner + b
            peer = self.hi * self.inner + lax.rem(self.lo + b, self.inner)
            self.arriving[a, b] = send(
                block, self.place(source_hi * self.inner + self.lo),
                self.s_sem.at[at], self.r_sem.at[at], {"fsdp": peer},
            )

    def across(self, a, b):
        if not self.over_tp:
            return
        halves = lax.axis_size("tp")
        tp = lax.axis_index("tp")
        source = lax.rem(self.hi + self.outer - a, self.outer) * self.inner + lax.rem(
            self.lo + self.inner - b, self.inner
        )
        block = self.place(source)
        for c in range(1, halves):
            at = (a * self.inner + b, c)
            self.sent.append(
                send(block, block, self.s_tp.at[at], self.r_tp.at[at], {"tp": lax.rem(tp + c, halves)})
            )

    def pass_on(self):
        self.pass_outer()
        self.pass_inner()

    def pass_outer(self):
        for a in range(1, self.outer):
            self.arriving[a, 0].wait_recv()
            source = lax.rem(self.hi + self.outer - a, self.outer) * self.inner + self.lo
            self.inward(a, self.place(source))
            self.across(a, 0)

    def pass_inner(self):
        for a in range(self.outer):
            for b in range(1, self.inner):
                self.arriving[a, b].wait_recv()
                self.across(a, b)

    def end(self):
        for copy in self.arriving.values():
            copy.wait_send()
        for copy in self.sent:
            copy.wait()


def chunks_of(rows):
    return 4 if rows % 64 == 0 else 2 if rows % 32 == 0 else 1


WINDOW = 6


def relay_kernel(
    split, base, codes, hidden, gain, got_base, got_codes, got_hidden, got_gain,
    s_base, r_base, s_fwd, r_fwd, s_code, r_code, s_hid, r_hid, s_htp, r_htp, s_gain, r_gain, s_local,
):
    groups, shards, halves = lax.axis_size("grp"), lax.axis_size("fsdp"), lax.axis_size("tp")
    grp, fsdp, tp = lax.axis_index("grp"), lax.axis_index("fsdp"), lax.axis_index("tp")
    width = base.shape[1]
    rows = base.shape[0] // shards
    part = rows // groups
    chunks = chunks_of(part)
    size = part // chunks
    code_rows = codes.shape[0]
    code_width = codes.shape[1] // halves
    hidden_part = hidden.shape[0] // halves
    outer, inner = folds(shards)
    greet(("grp", "fsdp", "tp"))

    hidden_rows = pl.ds(pl.multiple_of(tp * hidden_part, 16), hidden_part)
    spread = Spread(
        hidden.at[hidden_rows],
        lambda source: landing(got_hidden, split, hidden_rows, source, width),
        (s_hid, r_hid, s_htp, r_htp),
        True,
    )
    spread.begin()

    def my_rows(chunk, first):
        return pl.ds(pl.multiple_of(first + grp * part + chunk * size, 16), size)

    started = []
    plan = []
    hi, lo = fsdp // inner, lax.rem(fsdp, inner)
    for a in range(outer):
        for b in range(inner):
            if a == 0 and b == 0:
                continue
            peer = lax.rem(hi + a, outer) * inner + lax.rem(lo + b, inner)
            source = lax.rem(hi + outer - a, outer) * inner + lax.rem(lo + inner - b, inner)
            step = a * inner + b
            started.append(
                send(
                    gain, got_gain.at[fsdp], s_gain.at[step], r_gain.at[step], {"fsdp": peer}
                )
            )
            plan += [(step, chunk, peer, source) for chunk in range(chunks)]

    def send_base(step, chunk, peer, source):
        at = (step, chunk)
        return send(
            base.at[my_rows(chunk, peer * rows)],
            landing(got_base, split, my_rows(chunk, 0), fsdp, width),
            s_base.at[at], r_base.at[at], {"fsdp": peer},
        )

    flying = [send_base(*entry) for entry in plan[:WINDOW]]
    own_rows = pl.ds(pl.multiple_of(tp * code_rows, 16), code_rows)
    for step in range(1, halves):
        peer = lax.rem(tp + step, halves)
        started.append(
            send(
                codes.at[:, columns_at(peer, code_width)], got_codes.at[own_rows],
                s_code.at[step], r_code.at[step], {"tp": peer},
            )
        )
    local = [
        pltpu.make_async_copy(
            codes.at[:, columns_at(tp, code_width)], got_codes.at[own_rows], s_local.at[0]
        ),
        pltpu.make_async_copy(
            base.at[pl.ds(pl.multiple_of(fsdp * rows, 16), rows)],
            landing(got_base, split, pl.ds(0, rows), fsdp, width),
            s_local.at[1],
        ),
        pltpu.make_async_copy(
            hidden, landing(got_hidden, split, pl.ds(0, hidden.shape[0]), fsdp, width), s_local.at[2]
        ),
        pltpu.make_async_copy(gain, got_gain.at[fsdp], s_local.at[3]),
    ]
    for copy in local:
        copy.start()
    spread.pass_on()
    for index, (step, chunk, _, source) in enumerate(plan):
        copy = flying[index]
        copy.wait_send()
        if index + WINDOW < len(plan):
            flying.append(send_base(*plan[index + WINDOW]))
        copy.wait_recv()
        block = landing(got_base, split, my_rows(chunk, 0), source, width)
        for hop in range(1, groups):
            at = (step * chunks + chunk, hop)
            started.append(
                send(
                    block, block, s_fwd.at[at], r_fwd.at[at], {"grp": lax.rem(grp + hop, groups)}
                )
            )
    spread.end()
    for copy in started:
        copy.wait()
    for copy in local:
        copy.wait()


def relay(base, codes, hidden, gain, grp_size, shards, halves):
    width = base.shape[1]
    rows = base.shape[0] // shards
    chunks = chunks_of(rows // grp_size)
    split = width % 128 != 0

    def gathered(count):
        return (shards, count, width) if split else (count, shards * width)

    dma = pltpu.SemaphoreType.DMA
    got_base, got_codes, got_hidden, got_gain = pl.pallas_call(
        functools.partial(relay_kernel, split),
        out_shape=(
            jax.ShapeDtypeStruct(gathered(rows), base.dtype),
            jax.ShapeDtypeStruct((codes.shape[0] * halves, codes.shape[1] // halves), codes.dtype),
            jax.ShapeDtypeStruct(gathered(hidden.shape[0]), hidden.dtype),
            jax.ShapeDtypeStruct((shards, 1, width), gain.dtype),
        ),
        in_specs=[ANY] * 4,
        out_specs=(ANY,) * 4,
        scratch_shapes=[
            dma((shards, chunks)), dma((shards, chunks)),
            dma((shards * chunks, grp_size)), dma((shards * chunks, grp_size)),
            dma((halves,)), dma((halves,)),
            dma((shards,)), dma((shards,)), dma((shards, halves)), dma((shards, halves)),
            dma((shards,)), dma((shards,)), dma((4,)),
        ],
        compiler_params=pltpu.CompilerParams(collective_id=0, has_side_effects=True),
        cost_estimate=pl.CostEstimate(flops=0, bytes_accessed=250_000_000, transcendentals=0),
        name="relay",
    )(base, codes, hidden, gain[None])
    if split:
        got_base = jnp.swapaxes(got_base, 0, 1).reshape(rows, shards * width)
        got_hidden = jnp.swapaxes(got_hidden, 0, 1).reshape(-1, shards * width)
    return got_base, got_codes, got_hidden, got_gain.reshape(-1)


def gather_kernel(values, got, s_sem, r_sem, s_local):
    rows = values.shape[0]
    chunks = s_sem.shape[0]
    size = values.shape[1] // chunks
    greet(("fsdp",))

    def place(source, columns=slice(None)):
        return got.at[pl.ds(pl.multiple_of(source * rows, 16), rows), columns]

    spreads = []
    for chunk in range(chunks):
        columns = pl.ds(chunk * size, size)
        spreads.append(
            Spread(
                values.at[:, columns],
                functools.partial(place, columns=columns),
                (s_sem.at[chunk], r_sem.at[chunk], None, None),
                False,
            )
        )
    for spread in spreads[:2]:
        spread.begin()
    local = pltpu.make_async_copy(values, place(lax.axis_index("fsdp")), s_local)
    local.start()
    for chunk, spread in enumerate(spreads):
        spread.pass_outer()
        if chunk + 2 < chunks:
            spreads[chunk + 2].begin()
    for spread in spreads:
        spread.pass_inner()
        spread.end()
    local.wait()


def gather_rows(values, shards):
    chunks = 4 if values.shape[1] % 512 == 0 else 1
    dma = pltpu.SemaphoreType.DMA
    return pl.pallas_call(
        gather_kernel,
        out_shape=jax.ShapeDtypeStruct((values.shape[0] * shards, values.shape[1]), values.dtype),
        in_specs=[ANY],
        out_specs=ANY,
        scratch_shapes=[dma((chunks, shards)), dma((chunks, shards)), dma],
        compiler_params=pltpu.CompilerParams(collective_id=2, has_side_effects=True),
        name="gather_rows",
    )(values)


def to_rows_kernel(split, values, got, s_sem, r_sem, s_local):
    shards = lax.axis_size("fsdp")
    fsdp = lax.axis_index("fsdp")
    rows = values.shape[0] // shards
    width = values.shape[1]
    greet(("fsdp",))
    every = pl.ds(0, rows)
    copies = []
    for step in range(1, shards):
        peer = lax.rem(fsdp + step, shards)
        copy = pltpu.make_async_remote_copy(
            src_ref=values.at[pl.ds(pl.multiple_of(peer * rows, 8), rows)],
            dst_ref=landing(got, split, every, fsdp, width),
            send_sem=s_sem.at[step],
            recv_sem=r_sem.at[step],
            device_id={"fsdp": peer},
            device_id_type=MESH,
        )
        copy.start()
        copies.append(copy)
    local = pltpu.make_async_copy(
        values.at[pl.ds(pl.multiple_of(fsdp * rows, 8), rows)],
        landing(got, split, every, fsdp, width),
        s_local,
    )
    local.start()
    for copy in copies:
        copy.wait()
    local.wait()


def to_rows(values, shards):
    rows = values.shape[0] // shards
    width = values.shape[1]
    split = width % 128 != 0
    dma = pltpu.SemaphoreType.DMA
    got = pl.pallas_call(
        functools.partial(to_rows_kernel, split),
        out_shape=jax.ShapeDtypeStruct(
            (shards, rows, width) if split else (rows, shards * width), values.dtype
        ),
        in_specs=[ANY],
        out_specs=ANY,
        scratch_shapes=[dma((shards,)), dma((shards,)), dma],
        compiler_params=pltpu.CompilerParams(collective_id=1, has_side_effects=True),
        name="to_rows",
    )(values)
    if split:
        got = jnp.swapaxes(got, 0, 1).reshape(rows, shards * width)
    return got


def updated_matmul_kernel(x, base, codes, scale, out):
    depth = x.shape[1]

    @pl.when(pl.program_id(0) == 0)
    def _():
        out[...] = jnp.zeros_like(out)

    bands = scale.shape[0]
    height = base.shape[0] // bands
    columns = depth // BLOCK
    first = pl.program_id(0) * columns
    rows = []
    for band in range(bands):
        here = slice(band * height, (band + 1) * height)
        parts = []
        for block in range(columns):
            at = slice(block * BLOCK, (block + 1) * BLOCK)
            delta = codes[here, at].astype(jnp.float32) * scale[band, first + block]
            parts.append((base[here, at].astype(jnp.float32) + delta).astype(jnp.bfloat16))
        rows.append(jnp.concatenate(parts, axis=1))
    out[...] += lax.dot_general(
        x[...], jnp.concatenate(rows, axis=0), (((1,), (1,)), ((), ())),
        preferred_element_type=jnp.float32,
    )


def updated_matmul(x, base, codes, band_scale, depth=512):
    count, total = base.shape
    steps = total // depth
    return pl.pallas_call(
        updated_matmul_kernel,
        grid=(steps,),
        out_shape=jax.ShapeDtypeStruct((x.shape[0], count), jnp.float32),
        in_specs=[
            pl.BlockSpec((x.shape[0], depth), lambda i: (0, i)),
            pl.BlockSpec((count, depth), lambda i: (0, i)),
            pl.BlockSpec((count, depth), lambda i: (0, i)),
            pl.BlockSpec(memory_space=pltpu.SMEM),
        ],
        out_specs=pl.BlockSpec((x.shape[0], count), lambda i: (0, 0)),
        compiler_params=pltpu.CompilerParams(vmem_limit_bytes=56 * 2**20),
        cost_estimate=pl.CostEstimate(
            flops=2 * x.shape[0] * count * total, bytes_accessed=4 * count * total, transcendentals=0
        ),
        name="updated_matmul",
    )(x, base, codes, band_scale)


def band_scales(scale, first_row, rows):
    height = math.gcd(rows, BLOCK)
    ids = (first_row + height * jnp.arange(rows // height, dtype=jnp.int32)) // BLOCK
    pick = (ids[:, None] == jnp.arange(scale.shape[0], dtype=jnp.int32)[None, :]).astype(jnp.float32)
    return jnp.dot(pick, scale, precision=lax.Precision.HIGHEST)


def on_device(
    hidden,
    input_gain,
    q_gain,
    k_gain,
    base_qkv,
    codes_qkv,
    scale_qkv,
    base_out,
    codes_out,
    scale_out,
    lengths,
    key_cache,
    value_cache,
):
    grp_size, shards, halves = lax.axis_size("grp"), lax.axis_size("fsdp"), lax.axis_size("tp")
    fsdp_index = lax.axis_index("fsdp")
    tp_index = lax.axis_index("tp")
    row_count = hidden.shape[0]
    arrived_base, arrived_out, whole_hidden, whole_gain = relay(
        base_qkv, codes_out, hidden.reshape(row_count * 2, -1), input_gain, grp_size, shards, halves
    )

    hidden_float = whole_hidden.astype(jnp.float32)
    mean_square = jnp.sum(hidden_float * hidden_float, axis=-1) / D
    normed = (hidden_float * lax.rsqrt(mean_square + epsilon)[..., None] * whole_gain).astype(
        jnp.bfloat16
    )
    qkv_rows = codes_qkv.shape[0]
    qkv_scale = band_scales(scale_qkv, (tp_index * shards + fsdp_index) * qkv_rows, qkv_rows)
    projected = updated_matmul(normed, arrived_base, codes_qkv, qkv_scale)
    projected = to_rows(projected, shards).reshape(row_count // shards, 2, -1)
    attended = attend(projected, lengths, key_cache, value_cache, q_gain, k_gain)

    out_rows, out_columns = base_out.shape
    column_blocks = out_columns // BLOCK
    scale_columns = lax.dynamic_slice_in_dim(scale_out, tp_index * column_blocks, column_blocks, 1)
    out_scale = band_scales(scale_columns, fsdp_index * out_rows, out_rows)
    whole_attended = gather_rows(attended.reshape(-1, attended.shape[-1]), shards)
    partial_out = updated_matmul(whole_attended, base_out, arrived_out, out_scale)
    return lax.psum(partial_out, "tp").astype(jnp.bfloat16).reshape(row_count, 2, out_rows)


def solution(mesh):
    return jax.shard_map(
        on_device,
        mesh=mesh,
        in_specs=(
            P("grp", None, "fsdp"),
            P("fsdp"),
            P(),
            P(),
            P("tp", "fsdp"),
            P(("tp", "fsdp"), None),
            P(),
            P("fsdp", "tp"),
            P(("fsdp", "tp"), None),
            P(),
            P(("grp", "fsdp")),
            P(("grp", "fsdp"), None, "tp", None),
            P(("grp", "fsdp"), None, "tp", None),
        ),
        out_specs=P("grp", None, "fsdp"),
        check_vma=False,
    )
```

```python
import functools
import math

import jax
import jax.numpy as jnp
from jax import lax
from jax.experimental import pallas as pl
from jax.experimental.pallas import tpu as pltpu
from jax.sharding import PartitionSpec as P

D = 5120
BLOCK = 128


epsilon = 1e-06
rope_base = 1000000.0


def head_norm(values, gain):
    return values * lax.rsqrt(jnp.mean(values * values, axis=-1, keepdims=True) + epsilon) * gain


def rotate(values, positions):
    half_dim = values.shape[-1] // 2
    frequency = jnp.exp(
        jnp.arange(half_dim).astype(jnp.float32) * (-2.0 * math.log(rope_base) / values.shape[-1])
    )
    angles = positions.astype(jnp.float32)[..., None] * frequency
    angles = angles.reshape(
        positions.shape + (1,) * (values.ndim - positions.ndim - 1) + (half_dim,)
    )
    cosine = jnp.cos(angles)
    sine_part = jnp.sin(angles)
    first_part = values[..., :half_dim]
    second_part = values[..., half_dim:]
    return jnp.concatenate(
        [
            first_part * cosine - second_part * sine_part,
            second_part * cosine + first_part * sine_part,
        ],
        axis=-1,
    )


def attend(projected, lengths, key_cache, value_cache, q_gain, k_gain):
    row_count = projected.shape[0]
    groups = key_cache.shape[2]
    head_dim = key_cache.shape[3]
    grouped = projected.reshape(row_count, 2, groups, -1, head_dim)
    per_group = grouped.shape[3]
    queries = grouped[:, :, :, : per_group - 2]
    new_keys = grouped[:, :, :, per_group - 2]
    new_values = grouped[:, :, :, per_group - 1].astype(jnp.bfloat16)
    positions = lengths[:, None] + jnp.arange(2, dtype=jnp.int32)[None, :]
    queries = rotate(head_norm(queries, q_gain), positions).astype(jnp.bfloat16)
    new_keys = rotate(head_norm(new_keys, k_gain), positions).astype(jnp.bfloat16)
    scaling = 1.0 / math.sqrt(head_dim)
    cache_scores = (
        jnp.einsum("rsgqd,rlgd->rsgql", queries, key_cache, preferred_element_type=jnp.float32)
        * scaling
    )
    new_scores = (
        jnp.einsum("rsgqd,rtgd->rsgqt", queries, new_keys, preferred_element_type=jnp.float32)
        * scaling
    )
    cache_mask = (
        jnp.arange(key_cache.shape[1], dtype=jnp.int32)[None, :] < lengths[:, None]
    ).reshape(row_count, 1, 1, 1, -1)
    step_mask = (
        jnp.arange(2, dtype=jnp.int32)[None, :] <= jnp.arange(2, dtype=jnp.int32)[:, None]
    ).reshape(1, 2, 1, 1, 2)
    cache_weights = jnp.where(cache_mask, jnp.exp(cache_scores), 0.0)
    new_weights = jnp.where(step_mask, jnp.exp(new_scores), 0.0)
    totals = jnp.sum(cache_weights, axis=-1) + jnp.sum(new_weights, axis=-1)
    cache_weights = (cache_weights / totals[..., None]).astype(jnp.bfloat16)
    new_weights = (new_weights / totals[..., None]).astype(jnp.bfloat16)
    mixed = jnp.einsum(
        "rsgql,rlgd->rsgqd", cache_weights, value_cache, preferred_element_type=jnp.float32
    )
    mixed = mixed + jnp.einsum(
        "rsgqt,rtgd->rsgqd", new_weights, new_values, preferred_element_type=jnp.float32
    )
    return mixed.reshape(row_count, 2, -1).astype(jnp.bfloat16)


MESH = pl.DeviceIdType.MESH
ANY = pl.BlockSpec(memory_space=pl.ANY)


def greet(axes):
    barrier = pltpu.get_barrier_semaphore()
    total = 0
    for axis in axes:
        size = lax.axis_size(axis)
        me = lax.axis_index(axis)
        for step in range(1, size):
            pl.semaphore_signal(
                barrier, inc=1, device_id={axis: lax.rem(me + step, size)}, device_id_type=MESH
            )
        total += size - 1
    pl.semaphore_wait(barrier, total)


def columns_at(index, width):
    start = index * width
    return pl.ds(pl.multiple_of(start, 128) if width % 128 == 0 else start, width)


def landing(ref, split, rows, index, width):
    if split:
        return ref.at[index, rows]
    return ref.at[rows, columns_at(index, width)]


def folds(shards):
    inner = 2 if shards % 2 == 0 else 1
    return shards // inner, inner


def send(source, target, s_sem, r_sem, device):
    copy = pltpu.make_async_remote_copy(
        src_ref=source, dst_ref=target, send_sem=s_sem, recv_sem=r_sem,
        device_id=device, device_id_type=MESH,
    )
    copy.start()
    return copy


class Spread:
    def __init__(self, own, place, sems, over_tp):
        self.own, self.place, self.over_tp = own, place, over_tp
        self.s_sem, self.r_sem, self.s_tp, self.r_tp = sems
        self.shards = lax.axis_size("fsdp")
        self.outer, self.inner = folds(self.shards)
        fsdp = lax.axis_index("fsdp")
        self.hi, self.lo = fsdp // self.inner, lax.rem(fsdp, self.inner)
        self.arriving = {}
        self.sent = []

    def begin(self):
        fsdp = lax.axis_index("fsdp")
        for a in range(1, self.outer):
            at = a * self.inner
            peer = lax.rem(self.hi + a, self.outer) * self.inner + self.lo
            self.arriving[a, 0] = send(
                self.own, self.place(fsdp), self.s_sem.at[at], self.r_sem.at[at], {"fsdp": peer}
            )
        self.inward(0, self.own)

    def inward(self, a, block):
        source_hi = lax.rem(self.hi + self.outer - a, self.outer)
        for b in range(1, self.inner):
            at = a * self.inner + b
            peer = self.hi * self.inner + lax.rem(self.lo + b, self.inner)
            self.arriving[a, b] = send(
                block, self.place(source_hi * self.inner + self.lo),
                self.s_sem.at[at], self.r_sem.at[at], {"fsdp": peer},
            )

    def across(self, a, b):
        if not self.over_tp:
            return
        halves = lax.axis_size("tp")
        tp = lax.axis_index("tp")
        source = lax.rem(self.hi + self.outer - a, self.outer) * self.inner + lax.rem(
            self.lo + self.inner - b, self.inner
        )
        block = self.place(source)
        for c in range(1, halves):
            at = (a * self.inner + b, c)
            self.sent.append(
                send(block, block, self.s_tp.at[at], self.r_tp.at[at], {"tp": lax.rem(tp + c, halves)})
            )

    def pass_on(self):
        self.pass_outer()
        self.pass_inner()

    def pass_outer(self):
        for a in range(1, self.outer):
            self.arriving[a, 0].wait_recv()
            source = lax.rem(self.hi + self.outer - a, self.outer) * self.inner + self.lo
            self.inward(a, self.place(source))
            self.across(a, 0)

    def pass_inner(self):
        for a in range(self.outer):
            for b in range(1, self.inner):
                self.arriving[a, b].wait_recv()
                self.across(a, b)

    def end(self):
        for copy in self.arriving.values():
            copy.wait_send()
        for copy in self.sent:
            copy.wait()


def chunks_of(rows):
    return 4 if rows % 64 == 0 else 2 if rows % 32 == 0 else 1


WINDOW = 14


def relay_kernel(
    split, base, codes, hidden, gain, got_base, got_codes, got_hidden, got_gain,
    s_base, r_base, s_fwd, r_fwd, s_code, r_code, s_hid, r_hid, s_htp, r_htp, s_gain, r_gain, s_local,
):
    groups, shards, halves = lax.axis_size("grp"), lax.axis_size("fsdp"), lax.axis_size("tp")
    grp, fsdp, tp = lax.axis_index("grp"), lax.axis_index("fsdp"), lax.axis_index("tp")
    width = base.shape[1]
    rows = base.shape[0] // shards
    part = rows // groups
    chunks = chunks_of(part)
    size = part // chunks
    code_rows = codes.shape[0]
    code_width = codes.shape[1] // halves
    hidden_part = hidden.shape[0] // halves
    outer, inner = folds(shards)
    greet(("grp", "fsdp", "tp"))

    hidden_rows = pl.ds(pl.multiple_of(tp * hidden_part, 16), hidden_part)
    spread = Spread(
        hidden.at[hidden_rows],
        lambda source: landing(got_hidden, split, hidden_rows, source, width),
        (s_hid, r_hid, s_htp, r_htp),
        True,
    )
    spread.begin()

    def my_rows(chunk, first):
        return pl.ds(pl.multiple_of(first + grp * part + chunk * size, 16), size)

    started = []
    plan = []
    hi, lo = fsdp // inner, lax.rem(fsdp, inner)
    for a in range(outer):
        for b in range(inner):
            if a == 0 and b == 0:
                continue
            peer = lax.rem(hi + a, outer) * inner + lax.rem(lo + b, inner)
            source = lax.rem(hi + outer - a, outer) * inner + lax.rem(lo + inner - b, inner)
            step = a * inner + b
            started.append(
                send(
                    gain, got_gain.at[fsdp], s_gain.at[step], r_gain.at[step], {"fsdp": peer}
                )
            )
            plan += [(step, chunk, peer, source) for chunk in range(chunks)]

    def send_base(step, chunk, peer, source):
        at = (step, chunk)
        return send(
            base.at[my_rows(chunk, peer * rows)],
            landing(got_base, split, my_rows(chunk, 0), fsdp, width),
            s_base.at[at], r_base.at[at], {"fsdp": peer},
        )

    flying = [send_base(*entry) for entry in plan[:WINDOW]]
    own_rows = pl.ds(pl.multiple_of(tp * code_rows, 16), code_rows)
    for step in range(1, halves):
        peer = lax.rem(tp + step, halves)
        started.append(
            send(
                codes.at[:, columns_at(peer, code_width)], got_codes.at[own_rows],
                s_code.at[step], r_code.at[step], {"tp": peer},
            )
        )
    local = [
        pltpu.make_async_copy(
            codes.at[:, columns_at(tp, code_width)], got_codes.at[own_rows], s_local.at[0]
        ),
        pltpu.make_async_copy(
            base.at[pl.ds(pl.multiple_of(fsdp * rows, 16), rows)],
            landing(got_base, split, pl.ds(0, rows), fsdp, width),
            s_local.at[1],
        ),
        pltpu.make_async_copy(
            hidden, landing(got_hidden, split, pl.ds(0, hidden.shape[0]), fsdp, width), s_local.at[2]
        ),
        pltpu.make_async_copy(gain, got_gain.at[fsdp], s_local.at[3]),
    ]
    for copy in local:
        copy.start()
    spread.pass_on()
    for index, (step, chunk, _, source) in enumerate(plan):
        copy = flying[index]
        copy.wait_send()
        if index + WINDOW < len(plan):
            flying.append(send_base(*plan[index + WINDOW]))
        copy.wait_recv()
        block = landing(got_base, split, my_rows(chunk, 0), source, width)
        for hop in range(1, groups):
            at = (step * chunks + chunk, hop)
            started.append(
                send(
                    block, block, s_fwd.at[at], r_fwd.at[at], {"grp": lax.rem(grp + hop, groups)}
                )
            )
    spread.end()
    for copy in started:
        copy.wait()
    for copy in local:
        copy.wait()


def relay(base, codes, hidden, gain, grp_size, shards, halves):
    width = base.shape[1]
    rows = base.shape[0] // shards
    chunks = chunks_of(rows // grp_size)
    split = width % 128 != 0

    def gathered(count):
        return (shards, count, width) if split else (count, shards * width)

    dma = pltpu.SemaphoreType.DMA
    got_base, got_codes, got_hidden, got_gain = pl.pallas_call(
        functools.partial(relay_kernel, split),
        out_shape=(
            jax.ShapeDtypeStruct(gathered(rows), base.dtype),
            jax.ShapeDtypeStruct((codes.shape[0] * halves, codes.shape[1] // halves), codes.dtype),
            jax.ShapeDtypeStruct(gathered(hidden.shape[0]), hidden.dtype),
            jax.ShapeDtypeStruct((shards, 1, width), gain.dtype),
        ),
        in_specs=[ANY] * 4,
        out_specs=(ANY,) * 4,
        scratch_shapes=[
            dma((shards, chunks)), dma((shards, chunks)),
            dma((shards * chunks, grp_size)), dma((shards * chunks, grp_size)),
            dma((halves,)), dma((halves,)),
            dma((shards,)), dma((shards,)), dma((shards, halves)), dma((shards, halves)),
            dma((shards,)), dma((shards,)), dma((4,)),
        ],
        compiler_params=pltpu.CompilerParams(collective_id=0, has_side_effects=True),
        cost_estimate=pl.CostEstimate(flops=0, bytes_accessed=250_000_000, transcendentals=0),
        name="relay",
    )(base, codes, hidden, gain[None])
    if split:
        got_base = jnp.swapaxes(got_base, 0, 1).reshape(rows, shards * width)
        got_hidden = jnp.swapaxes(got_hidden, 0, 1).reshape(-1, shards * width)
    return got_base, got_codes, got_hidden, got_gain.reshape(-1)


def gather_kernel(values, got, s_sem, r_sem, s_local):
    rows = values.shape[0]
    chunks = s_sem.shape[0]
    size = values.shape[1] // chunks
    greet(("fsdp",))

    def place(source, columns=slice(None)):
        return got.at[pl.ds(pl.multiple_of(source * rows, 16), rows), columns]

    spreads = []
    for chunk in range(chunks):
        columns = pl.ds(chunk * size, size)
        spreads.append(
            Spread(
                values.at[:, columns],
                functools.partial(place, columns=columns),
                (s_sem.at[chunk], r_sem.at[chunk], None, None),
                False,
            )
        )
    for spread in spreads[:2]:
        spread.begin()
    local = pltpu.make_async_copy(values, place(lax.axis_index("fsdp")), s_local)
    local.start()
    for chunk, spread in enumerate(spreads):
        spread.pass_outer()
        if chunk + 2 < chunks:
            spreads[chunk + 2].begin()
    for spread in spreads:
        spread.pass_inner()
        spread.end()
    local.wait()


def gather_rows(values, shards):
    chunks = 4 if values.shape[1] % 512 == 0 else 1
    dma = pltpu.SemaphoreType.DMA
    return pl.pallas_call(
        gather_kernel,
        out_shape=jax.ShapeDtypeStruct((values.shape[0] * shards, values.shape[1]), values.dtype),
        in_specs=[ANY],
        out_specs=ANY,
        scratch_shapes=[dma((chunks, shards)), dma((chunks, shards)), dma],
        compiler_params=pltpu.CompilerParams(collective_id=2, has_side_effects=True),
        name="gather_rows",
    )(values)


def to_rows_kernel(split, values, got, s_sem, r_sem, s_local):
    shards = lax.axis_size("fsdp")
    fsdp = lax.axis_index("fsdp")
    rows = values.shape[0] // shards
    width = values.shape[1]
    greet(("fsdp",))
    every = pl.ds(0, rows)
    copies = []
    for step in range(1, shards):
        peer = lax.rem(fsdp + step, shards)
        copy = pltpu.make_async_remote_copy(
            src_ref=values.at[pl.ds(pl.multiple_of(peer * rows, 8), rows)],
            dst_ref=landing(got, split, every, fsdp, width),
            send_sem=s_sem.at[step],
            recv_sem=r_sem.at[step],
            device_id={"fsdp": peer},
            device_id_type=MESH,
        )
        copy.start()
        copies.append(copy)
    local = pltpu.make_async_copy(
        values.at[pl.ds(pl.multiple_of(fsdp * rows, 8), rows)],
        landing(got, split, every, fsdp, width),
        s_local,
    )
    local.start()
    for copy in copies:
        copy.wait()
    local.wait()


def to_rows(values, shards):
    rows = values.shape[0] // shards
    width = values.shape[1]
    split = width % 128 != 0
    dma = pltpu.SemaphoreType.DMA
    got = pl.pallas_call(
        functools.partial(to_rows_kernel, split),
        out_shape=jax.ShapeDtypeStruct(
            (shards, rows, width) if split else (rows, shards * width), values.dtype
        ),
        in_specs=[ANY],
        out_specs=ANY,
        scratch_shapes=[dma((shards,)), dma((shards,)), dma],
        compiler_params=pltpu.CompilerParams(collective_id=1, has_side_effects=True),
        name="to_rows",
    )(values)
    if split:
        got = jnp.swapaxes(got, 0, 1).reshape(rows, shards * width)
    return got


def updated_matmul_kernel(x, base, codes, scale, out):
    depth = x.shape[1]

    @pl.when(pl.program_id(0) == 0)
    def _():
        out[...] = jnp.zeros_like(out)

    bands = scale.shape[0]
    height = base.shape[0] // bands
    columns = depth // BLOCK
    first = pl.program_id(0) * columns
    rows = []
    for band in range(bands):
        here = slice(band * height, (band + 1) * height)
        parts = []
        for block in range(columns):
            at = slice(block * BLOCK, (block + 1) * BLOCK)
            delta = codes[here, at].astype(jnp.float32) * scale[band, first + block]
            parts.append((base[here, at].astype(jnp.float32) + delta).astype(jnp.bfloat16))
        rows.append(jnp.concatenate(parts, axis=1))
    out[...] += lax.dot_general(
        x[...], jnp.concatenate(rows, axis=0), (((1,), (1,)), ((), ())),
        preferred_element_type=jnp.float32,
    )


def updated_matmul(x, base, codes, band_scale, depth=512):
    count, total = base.shape
    steps = total // depth
    return pl.pallas_call(
        updated_matmul_kernel,
        grid=(steps,),
        out_shape=jax.ShapeDtypeStruct((x.shape[0], count), jnp.float32),
        in_specs=[
            pl.BlockSpec((x.shape[0], depth), lambda i: (0, i)),
            pl.BlockSpec((count, depth), lambda i: (0, i)),
            pl.BlockSpec((count, depth), lambda i: (0, i)),
            pl.BlockSpec(memory_space=pltpu.SMEM),
        ],
        out_specs=pl.BlockSpec((x.shape[0], count), lambda i: (0, 0)),
        compiler_params=pltpu.CompilerParams(vmem_limit_bytes=56 * 2**20),
        cost_estimate=pl.CostEstimate(
            flops=2 * x.shape[0] * count * total, bytes_accessed=4 * count * total, transcendentals=0
        ),
        name="updated_matmul",
    )(x, base, codes, band_scale)


def band_scales(scale, first_row, rows):
    height = math.gcd(rows, BLOCK)
    ids = (first_row + height * jnp.arange(rows // height, dtype=jnp.int32)) // BLOCK
    pick = (ids[:, None] == jnp.arange(scale.shape[0], dtype=jnp.int32)[None, :]).astype(jnp.float32)
    return jnp.dot(pick, scale, precision=lax.Precision.HIGHEST)


def on_device(
    hidden,
    input_gain,
    q_gain,
    k_gain,
    base_qkv,
    codes_qkv,
    scale_qkv,
    base_out,
    codes_out,
    scale_out,
    lengths,
    key_cache,
    value_cache,
):
    grp_size, shards, halves = lax.axis_size("grp"), lax.axis_size("fsdp"), lax.axis_size("tp")
    fsdp_index = lax.axis_index("fsdp")
    tp_index = lax.axis_index("tp")
    row_count = hidden.shape[0]
    arrived_base, arrived_out, whole_hidden, whole_gain = relay(
        base_qkv, codes_out, hidden.reshape(row_count * 2, -1), input_gain, grp_size, shards, halves
    )

    hidden_float = whole_hidden.astype(jnp.float32)
    mean_square = jnp.sum(hidden_float * hidden_float, axis=-1) / D
    normed = (hidden_float * lax.rsqrt(mean_square + epsilon)[..., None] * whole_gain).astype(
        jnp.bfloat16
    )
    qkv_rows = codes_qkv.shape[0]
    qkv_scale = band_scales(scale_qkv, (tp_index * shards + fsdp_index) * qkv_rows, qkv_rows)
    projected = updated_matmul(normed, arrived_base, codes_qkv, qkv_scale)
    projected = to_rows(projected, shards).reshape(row_count // shards, 2, -1)
    attended = attend(projected, lengths, key_cache, value_cache, q_gain, k_gain)

    out_rows, out_columns = base_out.shape
    column_blocks = out_columns // BLOCK
    scale_columns = lax.dynamic_slice_in_dim(scale_out, tp_index * column_blocks, column_blocks, 1)
    out_scale = band_scales(scale_columns, fsdp_index * out_rows, out_rows)
    whole_attended = gather_rows(attended.reshape(-1, attended.shape[-1]), shards)
    partial_out = updated_matmul(whole_attended, base_out, arrived_out, out_scale)
    return lax.psum(partial_out, "tp").astype(jnp.bfloat16).reshape(row_count, 2, out_rows)


def solution(mesh):
    return jax.shard_map(
        on_device,
        mesh=mesh,
        in_specs=(
            P("grp", None, "fsdp"),
            P("fsdp"),
            P(),
            P(),
            P("tp", "fsdp"),
            P(("tp", "fsdp"), None),
            P(),
            P("fsdp", "tp"),
            P(("fsdp", "tp"), None),
            P(),
            P(("grp", "fsdp")),
            P(("grp", "fsdp"), None, "tp", None),
            P(("grp", "fsdp"), None, "tp", None),
        ),
        out_specs=P("grp", None, "fsdp"),
        check_vma=False,
    )
```
